512 devices in a mesh: lon: 64 (over z_hi, y, core), lat: 8 (over x, z_lo).
Axes of the slice: x: 4, y: 8, z: 8 (z_hi: 4, z_lo: 2; z = z_hi * 2 + z_lo), core: 2. Of those that a mesh axis runs over, the one named last changes fastest.
Arguments:
- fields: bfloat16 [2, 48, 768, 192], P(None, 'lat', 'lon'), may hold values from -6 to 6
- grad_out: bfloat16 [2, 48, 768, 192], P(None, 'lat', 'lon'), may hold values from -6 to 6
- mask_ids: int32 [2, 48, 768], P(None, 'lat', 'lon'), may hold values from 0 to 2
- ln_gain: float32 [192], replicated, may hold values from 0.5 to 1.5
- qkv_weight: bfloat16 [192, 576], replicated, may hold values from -0.4375 to 0.4375
- proj_weight: bfloat16 [192, 192], replicated, may hold values from -0.4375 to 0.4375
- bias_table: float32 [8, 1, 6, 3312], P('lat'), may hold values from -6 to 6
Outputs:
- grad_fields: bfloat16 [2, 48, 768, 192], P(None, 'lat', 'lon')
- grad_qkv: float32 [192, 576], replicated
- grad_proj: float32 [192, 192], replicated
- grad_gain: float32 [192], replicated
- grad_table: float32 [8, 1, 6, 3312], P('lat')
The draws below stay inside these ranges and needn't reach their ends.
All inputs are finite; a program needn't handle non-finite values.
Results may differ from the reference program's by a relative error of at most 0.017.
Values may be sent and summed in bfloat16 or wider, within the bound.
A program may use at most 64 MiB of HBM per device.

```python
import jax
import jax.numpy as jnp
from jax import lax

D = 192
HEADS = 6
WIN_Z = 2
WIN_LAT = 6
WIN_LON = 12
LEVELS = 2
LAT = 48
LON = 768
LAT_WIN = 8
Z_WIN = 1
REL = 3312


def touch_ends(entries, stream_key, least, largest):
    shape = entries.shape
    place = [jax.random.randint(jax.random.fold_in(stream_key, axis), (), 0, shape[axis]) for axis in range(len(shape))]
    entries = entries.at[tuple(place)].set(least)
    longest = shape.index(max(shape))
    place[longest] = (place[longest] + 1) % shape[longest]
    return entries.at[tuple(place)].set(largest)


def block_scale(rng, dims, shards, smallest, largest):
    gain = 1.0
    for position, blocks in shards:
        steps = jax.random.uniform(jax.random.fold_in(jax.random.fold_in(rng, 6), position), (blocks,), jnp.float32, smallest / len(shards), largest / len(shards))
        gain = gain * jnp.repeat(jnp.exp(steps), dims[position] // blocks).reshape((-1,) + (1,) * (len(dims) - 1 - position))
    return gain


def normal_values(own_key, dims, spread, limit, cuts=(), kind=jnp.bfloat16):
    level = block_scale(own_key, dims, cuts, -0.22, 0.18) if cuts else 1.0
    values = jax.random.normal(own_key, dims, jnp.float32) * spread * level
    return jnp.minimum(jnp.maximum(values, -limit), limit).astype(kind)


def setup_inputs(seed: int = 0) -> dict:
    seeds = jax.random.split(jax.random.key(seed), 8)
    return {
        "fields": normal_values(seeds[0], (LEVELS, LAT, LON, D), 1.0, 6.0, ((1, 8), (2, 64))),
        "grad_out": normal_values(seeds[1], (LEVELS, LAT, LON, D), 1.0, 6.0, ((1, 8), (2, 64))),
        "mask_ids": touch_ends(jax.random.randint(seeds[2], (LEVELS, LAT, LON), 0, 3), jax.random.fold_in(seeds[2], 1), 0, 2).astype(jnp.int32),
        "ln_gain": jnp.clip(1.0 + 0.1 * jax.random.normal(seeds[3], (D,), jnp.float32), 0.5, 1.5),
        "qkv_weight": normal_values(seeds[4], (D, 3 * D), D ** -0.5, 0.4375),
        "proj_weight": normal_values(seeds[5], (D, D), D ** -0.5, 0.4375),
        "bias_table": normal_values(seeds[6], (LAT_WIN, Z_WIN, HEADS, REL), 1.0, 6.0, ((0, 8),), jnp.float32),
    }


epsilon = 1e-05

def to_windows(grid):
    level_count, row_count, col_count, channels = grid.shape
    shaped = grid.reshape(level_count // WIN_Z, WIN_Z, row_count // WIN_LAT, WIN_LAT, col_count // WIN_LON, WIN_LON, channels)
    shaped = shaped.transpose(2, 0, 4, 1, 3, 5, 6)
    return shaped.reshape(row_count // WIN_LAT, level_count // WIN_Z, col_count // WIN_LON, WIN_Z * WIN_LAT * WIN_LON, channels)

def from_windows(blocks, level_count, row_count, col_count):
    channels = blocks.shape[-1]
    shaped = blocks.reshape(row_count // WIN_LAT, level_count // WIN_Z, col_count // WIN_LON, WIN_Z, WIN_LAT, WIN_LON, channels)
    shaped = shaped.transpose(1, 3, 0, 4, 2, 5, 6)
    return shaped.reshape(level_count, row_count, col_count, channels)

def lon_pairs():
    shape = (WIN_LON, WIN_LON, 2 * WIN_LON - 1)
    first = lax.broadcasted_iota(jnp.int32, shape, 0)
    second = lax.broadcasted_iota(jnp.int32, shape, 1)
    offset = lax.broadcasted_iota(jnp.int32, shape, 2)
    return (second - first + WIN_LON - 1 == offset).astype(jnp.float32)

def window_grads(field_win, grad_win, ids_win, table_win, ln_gain, qkv_weight, proj_weight):
    win_count, win_tokens, channels = field_win.shape
    head_count = table_win.shape[1]
    head_size = channels // head_count
    floats = field_win.astype(jnp.float32)
    centred = floats - lax.optimization_barrier(jnp.mean(floats, axis=-1, keepdims=True))
    inv_std = lax.rsqrt(lax.optimization_barrier(jnp.mean(centred * centred, axis=-1, keepdims=True)) + epsilon)
    normed = centred * inv_std
    hidden = (normed * ln_gain).astype(jnp.bfloat16).reshape(win_count * win_tokens, channels)
    projected = jnp.dot(hidden, qkv_weight, preferred_element_type=jnp.float32)
    projected = projected.reshape(win_count, win_tokens, 3, head_count, head_size)
    scaling = head_size ** (-0.5)
    queries = (projected[:, :, 0] * scaling).astype(jnp.bfloat16)
    key_part = projected[:, :, 1].astype(jnp.bfloat16)
    value_part = projected[:, :, 2].astype(jnp.bfloat16)
    pairs = lon_pairs()
    table_shaped = table_win.reshape(win_count, head_count, WIN_Z, WIN_Z, WIN_LAT, WIN_LAT, 2 * WIN_LON - 1)
    bias_term = jnp.einsum('bhpqstr,ijr->bhpsiqtj', table_shaped.astype(jnp.float32), pairs)
    bias_term = bias_term.reshape(win_count, head_count, win_tokens, win_tokens)
    scores = jnp.einsum('bihd,bjhd->bhij', queries.astype(jnp.float32), key_part.astype(jnp.float32)) + bias_term
    same_id = ids_win[:, None, :, None] == ids_win[:, None, None, :]
    scores = jnp.where(same_id, scores, -1000000000.0)
    row_max = lax.optimization_barrier(jnp.max(scores, axis=-1, keepdims=True))
    raised = jnp.exp(scores - row_max)
    attn_prob = raised / lax.optimization_barrier(jnp.sum(raised, axis=-1, keepdims=True))
    prob_bf = attn_prob.astype(jnp.bfloat16)
    attended = jnp.einsum('bhij,bjhd->bihd', prob_bf.astype(jnp.float32), value_part.astype(jnp.float32))
    attended = attended.astype(jnp.bfloat16).reshape(win_count * win_tokens, channels)
    grad_flat = grad_win.reshape(win_count * win_tokens, channels)
    grad_proj = jnp.dot(attended.T, grad_flat, preferred_element_type=jnp.float32)
    grad_attended = jnp.dot(grad_flat, proj_weight.T, preferred_element_type=jnp.float32)
    grad_attended = grad_attended.astype(jnp.bfloat16).reshape(win_count, win_tokens, head_count, head_size)
    grad_prob = jnp.einsum('bihd,bjhd->bhij', grad_attended.astype(jnp.float32), value_part.astype(jnp.float32))
    grad_value = jnp.einsum('bhij,bihd->bjhd', prob_bf.astype(jnp.float32), grad_attended.astype(jnp.float32)).astype(jnp.bfloat16)
    grad_score = attn_prob * (grad_prob - lax.optimization_barrier(jnp.sum(attn_prob * grad_prob, axis=-1, keepdims=True)))
    score_shaped = grad_score.reshape(win_count, head_count, WIN_Z, WIN_LAT, WIN_LON, WIN_Z, WIN_LAT, WIN_LON)
    grad_table = jnp.einsum('bhpsiqtj,ijr->bhpqstr', score_shaped, pairs).reshape(win_count, head_count, -1)
    score_bf = grad_score.astype(jnp.bfloat16)
    grad_query = (jnp.einsum('bhij,bjhd->bihd', score_bf.astype(jnp.float32), key_part.astype(jnp.float32)) * scaling).astype(jnp.bfloat16)
    grad_key = jnp.einsum('bhij,bihd->bjhd', score_bf.astype(jnp.float32), queries.astype(jnp.float32)).astype(jnp.bfloat16)
    grad_joint = jnp.stack([grad_query, grad_key, grad_value], axis=2).reshape(win_count * win_tokens, 3 * channels)
    weight_grad = jnp.dot(hidden.T, grad_joint, preferred_element_type=jnp.float32)
    grad_hidden = jnp.dot(grad_joint, qkv_weight.T, preferred_element_type=jnp.float32).reshape(win_count, win_tokens, channels)
    grad_gain = lax.optimization_barrier(jnp.sum(grad_hidden * normed, axis=(0, 1)))
    scaled_grad = grad_hidden * ln_gain
    grad_local = inv_std * (scaled_grad - lax.optimization_barrier(jnp.mean(scaled_grad, axis=-1, keepdims=True)) - normed * lax.optimization_barrier(jnp.mean(scaled_grad * normed, axis=-1, keepdims=True)))
    return (grad_local.astype(jnp.bfloat16), weight_grad, grad_proj, grad_gain, grad_table)

def reference(fields, grad_out, mask_ids, ln_gain, qkv_weight, proj_weight, bias_table):
    shift_by = (-(WIN_Z // 2), -(WIN_LAT // 2), -(WIN_LON // 2))
    moved = to_windows(jnp.roll(fields, shift_by, (0, 1, 2)))
    moved_grad = to_windows(jnp.roll(grad_out, shift_by, (0, 1, 2)))
    ids_all = to_windows(mask_ids[..., None])[..., 0]
    lat_win, z_win, lon_win, win_tokens = moved.shape[:4]
    type_count = lat_win * z_win

    def per_type(pieces):
        field_win, grad_win, ids_win, table_row = pieces
        table_win = jnp.broadcast_to(table_row[None], (lon_win,) + table_row.shape)
        grad_local, weight_grad, grad_proj, grad_gain, grad_table = window_grads(field_win, grad_win, ids_win, table_win, ln_gain, qkv_weight, proj_weight)
        return (grad_local, weight_grad, grad_proj, grad_gain, lax.optimization_barrier(jnp.sum(grad_table, axis=0)))
    results = lax.map(per_type, (moved.reshape(type_count, lon_win, win_tokens, D), moved_grad.reshape(type_count, lon_win, win_tokens, D), ids_all.reshape(type_count, lon_win, win_tokens), bias_table.reshape(type_count, HEADS, REL)))
    grad_local, weight_grad, grad_proj, grad_gain, grad_table = results
    local_grid = from_windows(grad_local.reshape(lat_win, z_win, lon_win, win_tokens, D), LEVELS, LAT, LON)
    local_grid = jnp.roll(local_grid, (WIN_Z // 2, WIN_LAT // 2, WIN_LON // 2), (0, 1, 2))
    grad_fields = (grad_out.astype(jnp.float32) + local_grid.astype(jnp.float32)).astype(jnp.bfloat16)
    return (grad_fields, lax.optimization_barrier(jnp.sum(weight_grad, axis=0)), lax.optimization_barrier(jnp.sum(grad_proj, axis=0)), lax.optimization_barrier(jnp.sum(grad_gain, axis=0)), grad_table.reshape(bias_table.shape))
```

```python
import functools

import jax
import jax.numpy as jnp
import numpy as np
from jax import lax
from jax.experimental import pallas as pl
from jax.experimental.pallas import tpu as pltpu
from jax.sharding import PartitionSpec as P

D = 192
HEADS = 6
LON = 12
CELLS = 12
TOK = 144
SPAN = 23 * CELLS
SEG = 138
EPS = 1e-05
MESH = pl.DeviceIdType.MESH
BF = jnp.bfloat16
F32 = jnp.float32

NX, NY, NZH, NZL, NC = 4, 8, 4, 2, 2
GROUP = 8


def token_tables():
    gather = np.zeros((TOK, 384), np.float32)
    scatter = np.zeros((192, TOK), np.float32)
    for o in range(12):
        for z in range(2):
            for a in range(6):
                t = o * 12 + z * 6 + a
                s = (a >= 3) * 2 + (o >= 6)
                zs = (z + 1) % 2
                gather[t, s * 96 + (zs * 3 + a % 3) * 16 + (o + 6) % 12] = 1
                scatter[s * 48 + (zs * 3 + a % 3) * 6 + o % 6, t] = 1
    place = np.zeros((192, 192), np.float32)
    for z in range(2):
        for a in range(6):
            for o in range(12):
                s = (a < 3) * 2 + (o < 6)
                place[(z * 6 + a) * 16 + o, s * 48 + (z * 3 + a % 3) * 6 + o % 6] = 1
    shear = np.zeros((512, 384), np.float32)
    for zq in range(2):
        for aq in range(6):
            for r in range(23):
                shear[zq * 256 + aq * 23 + r, r * 12 + zq * 6 + aq] = 1
    row_of = np.zeros((TOK, 16), np.float32)
    lon_of = np.zeros((TOK, 128), np.float32)
    for t in range(TOK):
        row_of[t, t % 12] = 1
        lon_of[t, t // 12] = 1
    return gather, scatter, place, shear, row_of, lon_of


def dot(a, b):
    return lax.dot_general(a, b, (((1,), (0,)), ((), ())), preferred_element_type=F32)


def dot_rows(a, b):
    return lax.dot_general(a, b, (((1,), (1,)), ((), ())), preferred_element_type=F32)


def dot_cols(a, b):
    return lax.dot_general(a, b, (((0,), (0,)), ((), ())), preferred_element_type=F32)


def split(v):
    hi = v.astype(BF)
    return hi, (v - hi.astype(F32)).astype(BF)


def expand_bias(table, shear, xs, bias):
    for zp in range(2):
        for zq in range(2):
            for ap in range(6):
                start = ((zp * 2 + zq) * 6 + ap) * SEG
                rows = pl.ds(zp * 6 + ap, HEADS, stride=CELLS)
                part = table[0, 0, :, start : start + SEG]
                rest = jnp.concatenate([part[:, 128:], jnp.zeros((HEADS, 256 - SEG), F32)], axis=1)
                xs[2 * zq, rows, :] = part[:, 0:128]
                xs[2 * zq + 1, rows, :] = rest
    hi, lo = split(jnp.concatenate([xs[k] for k in range(4)], axis=1))
    sheared = dot(hi, shear[...]) + dot(lo, shear[...])
    for op in range(LON):
        window = sheared[:, (11 - op) * 12 : (11 - op) * 12 + TOK]
        for h in range(HEADS):
            bias[h, op * 12 : (op + 1) * 12, :] = window[h * 12 : (h + 1) * 12]


def fold_bias(gs, shear, stacked, xs, flat):
    for op in range(LON):
        for h in range(HEADS):
            stacked[op, h * 12 : (h + 1) * 12, :] = gs[h, op * 12 : (op + 1) * 12, :]
    total = None
    for op in range(LON):
        left = (11 - op) * 12
        parts = [stacked[op]]
        if left:
            parts.insert(0, jnp.zeros((72, left), F32))
        if SPAN - left - TOK:
            parts.append(jnp.zeros((72, SPAN - left - TOK), F32))
        piece = jnp.concatenate(parts, axis=1) if len(parts) > 1 else parts[0]
        total = piece if total is None else total + piece
    total = jnp.concatenate([total, jnp.zeros((72, 384 - SPAN), F32)], axis=1)
    hi, lo = split(total)
    spread = dot_rows(hi, shear[...]) + dot_rows(lo, shear[...])
    for k in range(4):
        xs[k] = spread[:, 128 * k : 128 * k + 128]
    for zp in range(2):
        for zq in range(2):
            for ap in range(6):
                start = ((zp * 2 + zq) * 6 + ap) * SEG
                rows = pl.ds(zp * 6 + ap, HEADS, stride=CELLS)
                flat[0:HEADS, start : start + 128] = xs[2 * zq, rows, :]
                flat[0:HEADS, start + 128 : start + SEG] = xs[2 * zq + 1, rows, :][:, 0 : SEG - 128]


def window_ids(ids, row_of, lon_of, ms):
    ms[...] = jnp.zeros_like(ms)
    ms[0:6, 0:12] = ids[0].astype(F32)
    ms[6:12, 0:12] = ids[1].astype(F32)
    m = ms[...].astype(BF)
    column = jnp.sum(dot(row_of[...], m) * lon_of[...].astype(F32), axis=1, keepdims=True)
    spread = dot_cols(m, row_of[...].astype(F32).T.astype(BF))
    row = jnp.sum(spread * lon_of[...].astype(F32).T, axis=0, keepdims=True)
    return column, row


def copy_slabs(received, s, slabs):
    for z in range(2):
        for a in range(3):
            row = (s * 6 + z * 3 + a) * 16
            slabs[row : row + 12, :] = received[s, z, a]


def window_grads(x, g, same, gain, wqkv, wproj, bias, gs_out):
    x = x.astype(F32)
    centred = x - jnp.mean(x, axis=-1, keepdims=True)
    inv_std = lax.rsqrt(jnp.mean(centred * centred, axis=-1, keepdims=True) + EPS)
    normed = centred * inv_std
    hidden = (normed * gain).astype(BF)
    projected = dot(hidden, wqkv)
    scaling = 32 ** (-0.5)
    query = (projected[:, :D] * scaling).astype(BF)
    key = projected[:, D : 2 * D].astype(BF)
    value = projected[:, 2 * D :].astype(BF)
    grad_att = dot_rows(g, wproj).astype(BF)
    lane = lax.broadcasted_iota(jnp.int32, (TOK, D), 1) // 32
    zero = jnp.zeros((TOK, D), BF)
    attended = dv = dq = dk = None

    def add(total, term):
        return term if total is None else total + term

    for h in range(HEADS):
        mine = lane == h
        qh = jnp.where(mine, query, zero)
        kh = jnp.where(mine, key, zero)
        vh = jnp.where(mine, value, zero)
        gh = jnp.where(mine, grad_att, zero)
        scores = jnp.where(same, dot_rows(qh, key) + bias[h], -1000000000.0)
        raised = jnp.exp(scores - jnp.max(scores, axis=-1, keepdims=True))
        prob = raised * (1.0 / jnp.sum(raised, axis=-1, keepdims=True))
        prob_bf = prob.astype(BF)
        attended = add(attended, dot(prob_bf, vh))
        grad_prob = dot_rows(gh, value)
        dv = add(dv, dot_cols(prob_bf, gh))
        weighted = prob * grad_prob
        gs = weighted - prob * jnp.sum(weighted, axis=-1, keepdims=True)
        gs_out[h] = gs
        gs = gs.astype(BF)
        dq = add(dq, dot(gs, kh))
        dk = add(dk, dot_cols(gs, qh))
    joint = jnp.concatenate(
        [(dq * scaling).astype(BF), dk.astype(BF), dv.astype(BF)], axis=1
    )
    grad_qkv = dot_cols(hidden, joint)
    grad_proj = dot_cols(attended.astype(BF), g)

    def local():
        grad_hidden = dot_rows(joint, wqkv)
        scaled = grad_hidden * gain
        return (
            inv_std
            * (
                scaled
                - jnp.mean(scaled, axis=-1, keepdims=True)
                - normed * jnp.mean(scaled * normed, axis=-1, keepdims=True)
            )
        ).astype(BF)

    return grad_qkv, grad_proj, local


def pack_weights(grad_qkv, grad_proj, flat):
    for c in range(4):
        flat[c * 192 : (c + 1) * 192, :] = grad_qkv[:, c * 128 : (c + 1) * 128].astype(BF)
    last = jnp.concatenate([grad_qkv[:, 512:576], grad_proj[:, 128:192]], axis=1)
    flat[768:960, :] = last.astype(BF)
    flat[960:1152, :] = grad_proj[:, 0:128].astype(BF)


def finish_weights(flat, wqkv, gain, out_qkv, out_proj, out_gain):
    for c in range(4):
        out_qkv[:, c * 128 : (c + 1) * 128] = flat[c * 192 : (c + 1) * 192, :].astype(F32)
    last = flat[768:960, :].astype(F32)
    out_qkv[:, 512:576] = last[:, 0:64]
    out_proj[:, 128:192] = last[:, 64:128]
    out_proj[:, 0:128] = flat[960:1152, :].astype(F32)
    products = out_qkv[...] * wqkv[...].astype(F32)
    hi, lo = split(products)
    ones = jnp.ones((8, 576), BF)
    row = (dot_rows(ones, hi) + dot_rows(ones, lo))[0:1]
    out_gain[...] = (row / gain[...].reshape(1, D)).reshape(D)


def finish_fields(quadrants, place, grad_out, out):
    blocks = dot(place[...], quadrants)
    for z in range(2):
        for a in range(6):
            row = (z * 6 + a) * 16
            own = grad_out[z, a].astype(F32)
            out[z, a] = (own + blocks[row : row + 12]).astype(BF)


def finish_table(rows, out):
    for k in range(26):
        width = min(128, 3312 - 128 * k)
        out[0, 0, :, 128 * k : 128 * k + width] = rows[8 * k : 8 * k + HEADS, 0:width].astype(F32)


def exchange(src_of, recv, rank, device_of, sends, recvs):
    copies = []
    for k in range(1, GROUP):
        peer = lax.rem(rank + k, GROUP)
        copy = pltpu.make_async_remote_copy(
            src_ref=src_of(peer),
            dst_ref=recv.at[rank],
            send_sem=sends.at[k],
            recv_sem=recvs.at[k],
            device_id=device_of(peer),
            device_id_type=MESH,
        )
        copy.start()
        copies.append(copy)
    return copies


def arrive(copies):
    for copy in copies:
        copy.wait_recv()


def total_of(recv):
    total = recv[0].astype(F32)
    for k in range(1, GROUP):
        total = total + recv[k].astype(F32)
    return total


def kernel(
    fields, grad_out, ids, gain, wqkv, wproj, table,
    gather, scatter, place, shear, row_of, lon_of,
    out_flat, out_quads, out_table,
    field_in, grad_in, slabs_f, slabs_g, xs, bias, gs, stacked, ms, tflat, quads_out, quads_in,
    w_out, w1, w2_out, w2, w3_out, w3, w4, w5,
    t1_out, t1, t2_out, t2, t3,
    own_sem, halo_send, halo_recv, back_send, back_recv, sends, recvs,
):
    l, a = lax.axis_index("lon"), lax.axis_index("lat")
    core, y, zh = lax.rem(l, NC), lax.rem(l // NC, NY), l // (NC * NY)
    x, zl = a // NZL, lax.rem(a, NZL)
    near_l, far_l = lax.rem(l + 63, 64), lax.rem(l + 1, 64)
    near_a, far_a = lax.rem(a + 7, 8), lax.rem(a + 1, 8)

    def lon(zh, y, core):
        return (zh * NY + y) * NC + core

    def by_xc(r):
        return (lon(zh, y, lax.rem(r, NC)), (r // NC) * NZL + zl)

    def by_y(r):
        return (lon(zh, r, core), a)

    def by_z(r):
        return (lon(r // NZL, y, core), x * NZL + lax.rem(r, NZL))

    def by_zc(r):
        return (lon(r // NC, y, lax.rem(r, NC)), a)

    groups = (
        (x * NC + core, by_xc),
        (y, by_y),
        (zh * NZL + zl, by_z),
        (zh * NC + core, by_zc),
    )
    barrier = pltpu.get_barrier_semaphore()
    near = ((near_l, a), (l, near_a), (near_l, near_a))
    far = ((far_l, a), (l, far_a), (far_l, far_a))
    for device in near + far:
        pl.semaphore_signal(barrier, inc=1, device_id=device, device_id_type=MESH)
    for rank, device_of in groups:
        for k in range(1, GROUP):
            pl.semaphore_signal(
                barrier, inc=1, device_id=device_of(lax.rem(rank + k, GROUP)), device_id_type=MESH
            )
    owns = []
    for k, (src, dst) in enumerate(((fields, field_in), (grad_out, grad_in))):
        own = pltpu.make_async_copy(src.at[:, 3:6], dst.at[0], own_sem.at[k])
        own.start()
        owns.append(own)
    pl.semaphore_wait(barrier, 6 + 7 * len(groups))

    halo = []
    for s in range(1, 4):
        rows = slice(3, 6) if s == 1 else slice(0, 3)
        for k, (src, dst) in enumerate(((fields, field_in), (grad_out, grad_in))):
            copy = pltpu.make_async_remote_copy(
                src_ref=src.at[:, rows],
                dst_ref=dst.at[s],
                send_sem=halo_send.at[2 * s + k],
                recv_sem=halo_recv.at[2 * s + k],
                device_id=near[s - 1],
                device_id_type=MESH,
            )
            copy.start()
            halo.append(copy)

    slabs_f[...] = jnp.zeros_like(slabs_f)
    slabs_g[...] = jnp.zeros_like(slabs_g)
    expand_bias(table, shear, xs, bias)
    column, row = window_ids(ids, row_of, lon_of, ms)
    same = column == row

    for own in owns:
        own.wait()
    copy_slabs(field_in, 0, slabs_f)
    copy_slabs(grad_in, 0, slabs_g)
    arrive(halo)
    for s in range(1, 4):
        copy_slabs(field_in, s, slabs_f)
        copy_slabs(grad_in, s, slabs_g)
    moved = dot(gather[...], slabs_f[...]).astype(BF)
    moved_grad = dot(gather[...], slabs_g[...]).astype(BF)
    grad_qkv, grad_proj, local = window_grads(
        moved, moved_grad, same, gain[...].reshape(1, D), wqkv[...], wproj[...], bias, gs
    )

    pack_weights(grad_qkv, grad_proj, w_out)
    started = []

    def go(index, src_of, recv, group, local_src):
        rank, device_of = groups[group]
        copies = exchange(src_of, recv, rank, device_of, sends.at[index], recvs.at[index])
        started.extend(copies)
        recv[rank] = local_src(rank)
        return copies

    def block(ref, size):
        return lambda r: ref.at[pl.ds(pl.multiple_of(r * size, size), size)]

    def block_value(ref, size):
        return lambda r: ref[pl.ds(pl.multiple_of(r * size, size), size), :]

    c1 = go(0, block(w_out, 144), w1, 0, block_value(w_out, 144))

    quads = dot(scatter[...], local()).astype(BF)
    quads_out[...] = quads.reshape(4, 48, D)
    back = []
    for s in range(1, 4):
        copy = pltpu.make_async_remote_copy(
            src_ref=quads_out.at[s],
            dst_ref=quads_in.at[s],
            send_sem=back_send.at[s],
            recv_sem=back_recv.at[s],
            device_id=far[s - 1],
            device_id_type=MESH,
        )
        copy.start()
        back.append(copy)
    quads_in[0] = quads_out[0]

    tflat[...] = jnp.zeros_like(tflat)
    fold_bias(gs, shear, stacked, xs, tflat)
    rows = jnp.concatenate([tflat[:, 128 * k : 128 * (k + 1)] for k in range(26)], axis=0)
    t1_out[0:208, :] = rows.astype(BF)
    t1_out[208:256, :] = jnp.zeros((48, 128), BF)
    d1 = go(1, block(t1_out, 32), t1, 1, block_value(t1_out, 32))

    arrive(c1)
    sum1 = total_of(w1).astype(BF)
    for k in range(8):
        w2_out[k, 0:16] = sum1[16 * k : 16 * k + 16]
        w2_out[k, 16:32] = sum1[128:144] if k == 0 else jnp.zeros((16, 128), BF)
    c2 = go(2, lambda r: w2_out.at[r], w2, 1, lambda r: w2_out[r])

    arrive(d1)
    t2_out[...] = total_of(t1).astype(BF)
    d2 = go(3, lambda r: t2_out, t2, 3, lambda r: t2_out[...])

    arrive(c2)
    w3_out[...] = total_of(w2).astype(BF)
    c3 = go(4, lambda r: w3_out, w3, 2, lambda r: w3_out[...])

    arrive(d2)
    t2_out2 = total_of(t2).astype(BF)
    rank_y = groups[1][0]
    t3[rank_y] = t2_out2
    d3 = exchange(lambda r: t3.at[rank_y], t3, rank_y, by_y, sends.at[5], recvs.at[5])
    started.extend(d3)

    arrive(c3)
    w4[rank_y] = total_of(w3).astype(BF)
    c4 = exchange(lambda r: w4.at[rank_y], w4, rank_y, by_y, sends.at[6], recvs.at[6])
    started.extend(c4)
    arrive(c4)
    rank_xc = groups[0][0]
    for k in range(8):
        w5[rank_xc, 16 * k : 16 * k + 16] = w4[k, 0:16]
    w5[rank_xc, 128:144] = w4[0, 16:32]
    c5 = exchange(lambda r: w5.at[rank_xc], w5, rank_xc, by_xc, sends.at[7], recvs.at[7])
    started.extend(c5)

    arrive(d3)
    for k in range(8):
        out_table[32 * k : 32 * k + 32, :] = t3[k]
    arrive(back)
    out_quads[...] = quads_in[...].reshape(192, D)
    arrive(c5)
    for k in range(8):
        out_flat[144 * k : 144 * k + 144, :] = w5[k]
    for copy in halo + back + started:
        copy.wait_send()


def finish(flat, quads, trows, grad_out, place, wqkv, gain, out_f, out_qkv, out_proj, out_gain, out_t):
    finish_weights(flat, wqkv, gain, out_qkv, out_proj, out_gain)
    finish_fields(quads[...], place, grad_out, out_f)
    finish_table(trows, out_t)


def body(fields, grad_out, mask_ids, ln_gain, qkv_weight, proj_weight, bias_table):
    consts = [jnp.asarray(v, BF) for v in token_tables()]
    vmem = pl.BlockSpec(memory_space=pltpu.VMEM)
    hbm = pl.BlockSpec(memory_space=pl.ANY)
    dma = pltpu.SemaphoreType.DMA
    scratch = [
        pltpu.VMEM((4, 2, 3, 12, D), BF),
        pltpu.VMEM((4, 2, 3, 12, D), BF),
        pltpu.VMEM((384, D), BF),
        pltpu.VMEM((384, D), BF),
        pltpu.VMEM((4, 72, 128), F32),
        pltpu.VMEM((HEADS, TOK, TOK), F32),
        pltpu.VMEM((HEADS, TOK, TOK), F32),
        pltpu.VMEM((LON, 72, TOK), F32),
        pltpu.VMEM((16, 128), F32),
        pltpu.VMEM((8, 3328), F32),
        pltpu.VMEM((4, 48, D), BF),
        pltpu.VMEM((4, 48, D), BF),
        pltpu.VMEM((1152, 128), BF),
        pltpu.VMEM((8, 144, 128), BF),
        pltpu.VMEM((8, 32, 128), BF),
        pltpu.VMEM((8, 32, 128), BF),
        pltpu.VMEM((32, 128), BF),
        pltpu.VMEM((8, 32, 128), BF),
        pltpu.VMEM((8, 32, 128), BF),
        pltpu.VMEM((8, 144, 128), BF),
        pltpu.VMEM((256, 128), BF),
        pltpu.VMEM((8, 32, 128), BF),
        pltpu.VMEM((32, 128), BF),
        pltpu.VMEM((8, 32, 128), BF),
        pltpu.VMEM((8, 32, 128), BF),
        dma((2,)),
        dma((8,)),
        dma((8,)),
        dma((4,)),
        dma((4,)),
        dma((8, 8)),
        dma((8, 8)),
    ]
    flat, quads, trows = pl.pallas_call(
        kernel,
        out_shape=(
            jax.ShapeDtypeStruct((1152, 128), BF),
            jax.ShapeDtypeStruct((192, D), BF),
            jax.ShapeDtypeStruct((256, 128), BF),
        ),
        in_specs=[hbm, hbm] + [vmem] * 11,
        out_specs=(vmem, vmem, vmem),
        scratch_shapes=scratch,
        compiler_params=pltpu.CompilerParams(
            collective_id=0, has_side_effects=True, vmem_limit_bytes=32 * 1024 * 1024
        ),
    )(fields, grad_out, mask_ids, ln_gain, qkv_weight, proj_weight, bias_table, *consts)
    place = consts[2]
    out_f, out_qkv, out_proj, out_gain, out_t = pl.pallas_call(
        finish,
        out_shape=(
            jax.ShapeDtypeStruct((2, 6, 12, D), BF),
            jax.ShapeDtypeStruct((D, 576), F32),
            jax.ShapeDtypeStruct((D, D), F32),
            jax.ShapeDtypeStruct((D,), F32),
            jax.ShapeDtypeStruct((1, 1, HEADS, 3312), F32),
        ),
        in_specs=[vmem] * 7,
        out_specs=(vmem,) * 5,
        compiler_params=pltpu.CompilerParams(vmem_limit_bytes=32 * 1024 * 1024),
    )(flat, quads, trows, grad_out, place, qkv_weight, ln_gain)
    return out_f, out_qkv, out_proj, out_gain, out_t


def solution(mesh):
    placed = (
        P(None, "lat", "lon", None),
        P(None, "lat", "lon", None),
        P(None, "lat", "lon"),
        P(),
        P(),
        P(),
        P("lat", None, None, None),
    )
    return jax.shard_map(
        body,
        mesh=mesh,
        in_specs=placed,
        out_specs=(P(None, "lat", "lon", None), P(), P(), P(), P("lat", None, None, None)),
        check_vma=False,
    )
```

```python
import functools

import jax
import jax.numpy as jnp
import numpy as np
from jax import lax
from jax.experimental import pallas as pl
from jax.experimental.pallas import tpu as pltpu
from jax.sharding import PartitionSpec as P

D = 192
HEADS = 6
LON = 12
CELLS = 12
TOK = 144
SPAN = 23 * CELLS
SEG = 138
EPS = 1e-05
MESH = pl.DeviceIdType.MESH
BF = jnp.bfloat16
F32 = jnp.float32

INSIDE, ACROSS, FOUR = 16, 16, 4
ROWS = 1152 // (2 * INSIDE)
VMEM_LIMIT = 60 * 1024 * 1024


def token_tables():
    gather = np.zeros((TOK, TOK), np.float32)
    for o in range(12):
        for z in range(2):
            for a in range(6):
                s = (a >= 3) * 2 + (o >= 6)
                gather[o * 12 + z * 6 + a, ((s * 3 + a % 3) * 6 + o % 6) * 2 + (z + 1) % 2] = 1
    shear = np.zeros((512, 384), np.float32)
    for zq in range(2):
        for aq in range(6):
            for r in range(23):
                shear[zq * 256 + aq * 23 + r, r * 12 + zq * 6 + aq] = 1
    row_of = np.zeros((TOK, 16), np.float32)
    lon_of = np.zeros((TOK, 128), np.float32)
    for t in range(TOK):
        row_of[t, t % 12] = 1
        lon_of[t, t // 12] = 1
    return gather, shear, row_of, lon_of


def dot(a, b):
    return lax.dot_general(a, b, (((1,), (0,)), ((), ())), preferred_element_type=F32)


def dot_rows(a, b):
    return lax.dot_general(a, b, (((1,), (1,)), ((), ())), preferred_element_type=F32)


def dot_cols(a, b):
    return lax.dot_general(a, b, (((0,), (0,)), ((), ())), preferred_element_type=F32)


def split(v):
    hi = v.astype(BF)
    return hi, (v - hi.astype(F32)).astype(BF)


def expand_bias(table, shear, xs, bias):
    for zp in range(2):
        for zq in range(2):
            for ap in range(6):
                start = ((zp * 2 + zq) * 6 + ap) * SEG
                rows = pl.ds(zp * 6 + ap, HEADS, stride=CELLS)
                part = table[:, 0, start : start + SEG]
                rest = jnp.concatenate([part[:, 128:], jnp.zeros((HEADS, 256 - SEG), F32)], axis=1)
                xs[2 * zq, rows, :] = part[:, 0:128]
                xs[2 * zq + 1, rows, :] = rest
    hi, lo = split(jnp.concatenate([xs[k] for k in range(4)], axis=1))
    sheared = dot(hi, shear[...]) + dot(lo, shear[...])
    for op in range(LON):
        window = sheared[:, (11 - op) * 12 : (11 - op) * 12 + TOK]
        for h in range(HEADS):
            bias[h, op * 12 : (op + 1) * 12, :] = window[h * 12 : (h + 1) * 12]


def fold_bias(gs, shear, stacked, xs, flat):
    for op in range(LON):
        for h in range(HEADS):
            stacked[op, h * 12 : (h + 1) * 12, :] = gs[h, op * 12 : (op + 1) * 12, :]
    total = None
    for op in range(LON):
        left = (11 - op) * 12
        parts = [stacked[op]]
        if left:
            parts.insert(0, jnp.zeros((72, left), F32))
        if SPAN - left - TOK:
            parts.append(jnp.zeros((72, SPAN - left - TOK), F32))
        piece = jnp.concatenate(parts, axis=1) if len(parts) > 1 else parts[0]
        total = piece if total is None else total + piece
    total = jnp.concatenate([total, jnp.zeros((72, 384 - SPAN), F32)], axis=1)
    hi, lo = split(total)
    spread = dot_rows(hi, shear[...]) + dot_rows(lo, shear[...])
    for k in range(4):
        xs[k] = spread[:, 128 * k : 128 * k + 128]
    for zp in range(2):
        for zq in range(2):
            for ap in range(6):
                start = ((zp * 2 + zq) * 6 + ap) * SEG
                rows = pl.ds(zp * 6 + ap, HEADS, stride=CELLS)
                flat[0:HEADS, start : start + 128] = xs[2 * zq, rows, :]
                flat[0:HEADS, start + 128 : start + SEG] = xs[2 * zq + 1, rows, :][:, 0 : SEG - 128]


def window_ids(ids, row_of, lon_of, ms):
    ms[...] = jnp.zeros_like(ms)
    for a in range(6):
        ms[a : a + 1, 0:12] = ids[a, 0:1].astype(F32)
        ms[a + 6 : a + 7, 0:12] = ids[a, 1:2].astype(F32)
    m = ms[...].astype(BF)
    column = jnp.sum(dot(row_of[...], m) * lon_of[...].astype(F32), axis=1, keepdims=True)
    spread = dot_cols(m, row_of[...].astype(F32).T.astype(BF))
    row = jnp.sum(spread * lon_of[...].astype(F32).T, axis=0, keepdims=True)
    return column, row


def window_grads(x, g, same, gain, wqkv, wproj, bias, gs_out):
    x = x.astype(F32)
    centred = x - jnp.mean(x, axis=-1, keepdims=True)
    inv_std = lax.rsqrt(jnp.mean(centred * centred, axis=-1, keepdims=True) + EPS)
    normed = centred * inv_std
    hidden = (normed * gain).astype(BF)
    projected = dot(hidden, wqkv)
    scaling = 32 ** (-0.5)
    query = (projected[:, :D] * scaling).astype(BF)
    key = projected[:, D : 2 * D].astype(BF)
    value = projected[:, 2 * D :].astype(BF)
    grad_att = dot_rows(g, wproj).astype(BF)
    lane = lax.broadcasted_iota(jnp.int32, (TOK, D), 1) // 32
    zero = jnp.zeros((TOK, D), BF)
    attended = dv = dq = dk = None

    def add(total, term):
        return term if total is None else total + term

    for h in range(HEADS):
        mine = lane == h
        qh = jnp.where(mine, query, zero)
        kh = jnp.where(mine, key, zero)
        vh = jnp.where(mine, value, zero)
        gh = jnp.where(mine, grad_att, zero)
        scores = jnp.where(same, dot_rows(qh, key) + bias[h], -1000000000.0)
        raised = jnp.exp(scores - jnp.max(scores, axis=-1, keepdims=True))
        prob = raised * (1.0 / jnp.sum(raised, axis=-1, keepdims=True))
        prob_bf = prob.astype(BF)
        attended = add(attended, dot(prob_bf, vh))
        grad_prob = dot_rows(gh, value)
        dv = add(dv, dot_cols(prob_bf, gh))
        weighted = prob * grad_prob
        gs = weighted - prob * jnp.sum(weighted, axis=-1, keepdims=True)
        gs_out[h] = gs
        gs = gs.astype(BF)
        dq = add(dq, dot(gs, kh))
        dk = add(dk, dot_cols(gs, qh))
    joint = jnp.concatenate(
        [(dq * scaling).astype(BF), dk.astype(BF), dv.astype(BF)], axis=1
    )
    grad_qkv = dot_cols(hidden, joint)
    grad_proj = dot_cols(attended.astype(BF), g)

    def local():
        grad_hidden = dot_rows(joint, wqkv)
        scaled = grad_hidden * gain
        return (
            inv_std
            * (
                scaled
                - jnp.mean(scaled, axis=-1, keepdims=True)
                - normed * jnp.mean(scaled * normed, axis=-1, keepdims=True)
            )
        ).astype(BF)

    return grad_qkv, grad_proj, local


def pack_weights(grad_qkv, grad_proj, flat, out):
    for c in range(4):
        flat[c * 192 : (c + 1) * 192, :] = grad_qkv[:, c * 128 : (c + 1) * 128]
    flat[768:960, :] = jnp.concatenate([grad_qkv[:, 512:576], grad_proj[:, 128:192]], axis=1)
    flat[960:1152, :] = grad_proj[:, 0:128]
    for r in range(2 * INSIDE):
        out[r // INSIDE, r % INSIDE] = flat[ROWS * r : ROWS * (r + 1), :].astype(BF)


def finish_weights(rows, wqkv, gain, flat, out_qkv, out_proj, out_gain):
    for r in range(2 * INSIDE):
        flat[ROWS * r : ROWS * (r + 1), :] = rows[r // INSIDE, r % INSIDE].astype(F32)
    for c in range(4):
        out_qkv[:, c * 128 : (c + 1) * 128] = flat[c * 192 : (c + 1) * 192, :]
    last = flat[768:960, :]
    out_qkv[:, 512:576] = last[:, 0:64]
    out_proj[:, 128:192] = last[:, 64:128]
    out_proj[:, 0:128] = flat[960:1152, :]
    products = out_qkv[...] * wqkv[...].astype(F32)
    hi, lo = split(products)
    ones = jnp.ones((8, 576), BF)
    row = (dot_rows(ones, hi) + dot_rows(ones, lo))[0:1]
    out_gain[...] = (row / gain[...].reshape(1, D)).reshape(D)


def finish_fields(quads, grad_out, out):
    for s in range(4):
        rows = slice(0, 3) if s >= 2 else slice(3, 6)
        cols = slice(0, 6) if s % 2 else slice(6, 12)
        out[rows, cols] = (grad_out[rows, cols].astype(F32) + quads[s].astype(F32)).astype(BF)


def finish_table(rows, out):
    for k in range(26):
        width = min(128, 3312 - 128 * k)
        block = rows[k // 2].astype(F32)[8 * (k % 2) : 8 * (k % 2) + 8]
        for h in range(HEADS):
            out[h, :, 128 * k : 128 * k + width] = block[h : h + 1, 0:width]


def exchange(src_of, recv, group, sends, recvs):
    size, rank, device_of = group
    copies = []
    for k in range(1, size):
        peer = lax.rem(rank + k, size)
        copy = pltpu.make_async_remote_copy(
            src_ref=src_of(peer),
            dst_ref=recv.at[rank],
            send_sem=sends.at[k],
            recv_sem=recvs.at[k],
            device_id=device_of(peer),
            device_id_type=MESH,
        )
        copy.start()
        copies.append(copy)
    return copies


def arrive(copies):
    for copy in copies:
        copy.wait_recv()


def total_of(recv):
    total = recv[0].astype(F32)
    for k in range(1, recv.shape[0]):
        total = total + recv[k].astype(F32)
    return total


def kernel(
    fields, grad_out, ids_hbm, gain_hbm, wqkv_hbm, wproj_hbm, table_hbm,
    gather_hbm, shear_hbm, row_hbm, lon_hbm,
    out_flat, out_quads, out_table,
    ids, gain, wqkv, wproj, table, gather, shear, row_of, lon_of,
    field_in, grad_in, xs, bias, gs, stacked, ms, tflat, quads_out, quads_in,
    flat, w_out, w_in, w_half, w1, w2_out, w2, w3, t_out, t1, t2_out, t2, t3,
    block_sem, across_sem, load_sem, own_sem, halo_send, halo_recv, back_send, back_recv,
    pair_send, pair_recv, w1_send, w1_recv, w2_send, w2_recv, w3_send, w3_recv, w4_send, w4_recv,
    t1_send, t1_recv, t2_send, t2_recv, t3_send, t3_recv,
):
    l, a = lax.axis_index("lon"), lax.axis_index("lat")
    part, block = lax.rem(l, FOUR), l // FOUR
    core, side = lax.rem(part, 2), part // 2
    near_l, far_l = lax.rem(l + 63, 64), lax.rem(l + 1, 64)
    near_a, far_a = lax.rem(a + 7, 8), lax.rem(a + 1, 8)

    inside = (INSIDE, a * 2 + side, lambda r: (block * FOUR + lax.rem(r, 2) * 2 + core, r // 2))
    across = (ACROSS, block, lambda r: (r * FOUR + part, a))
    in_four = (FOUR, part, lambda r: (block * FOUR + r, a))
    barrier = pltpu.get_barrier_semaphore()
    near = ((near_l, a), (l, near_a), (near_l, near_a))
    far = ((far_l, a), (l, far_a), (far_l, far_a))
    beside = [(near_l, a), (far_l, a), near[2], far[2]]
    column = [(l, lax.rem(a + k, 8)) for k in range(1, 8)]
    four = [(block * FOUR + lax.rem(part + k, FOUR), a) for k in range(1, FOUR)]
    high, low = block // 4, lax.rem(block, 4)
    lows = [((high * 4 + lax.rem(low + k, 4)) * FOUR + part, a) for k in range(1, 4)]
    highs = [((lax.rem(high + k, 4) * 4 + low) * FOUR + part, a) for k in range(1, 4)]
    entry = beside + column + four + lows + highs
    for device in entry:
        pl.semaphore_signal(barrier, inc=1, device_id=device, device_id_type=MESH)
    loads = []
    pairs = (
        (table_hbm, table), (shear_hbm, shear), (ids_hbm, ids), (row_hbm, row_of), (lon_hbm, lon_of),
        (gather_hbm, gather), (gain_hbm, gain), (wqkv_hbm, wqkv), (wproj_hbm, wproj),
    )
    for k, (src, dst) in enumerate(pairs):
        load = pltpu.make_async_copy(src, dst, load_sem.at[k])
        load.start()
        loads.append(load)
    owns = []
    for k, (src, dst) in enumerate(((fields, field_in), (grad_out, grad_in))):
        own = pltpu.make_async_copy(src.at[3:6, 6:12], dst.at[0], own_sem.at[k])
        own.start()
        owns.append(own)
    pl.semaphore_wait(barrier, len(entry))

    halo = []
    for s in range(1, 4):
        rows = slice(0, 3) if s >= 2 else slice(3, 6)
        cols = slice(0, 6) if s % 2 else slice(6, 12)
        for k, (src, dst) in enumerate(((fields, field_in), (grad_out, grad_in))):
            copy = pltpu.make_async_remote_copy(
                src_ref=src.at[rows, cols],
                dst_ref=dst.at[s],
                send_sem=halo_send.at[2 * s + k],
                recv_sem=halo_recv.at[2 * s + k],
                device_id=near[s - 1],
                device_id_type=MESH,
            )
            copy.start()
            halo.append(copy)

    for device in four:
        pl.semaphore_signal(block_sem, inc=1, device_id=device, device_id_type=MESH)
    for device in highs:
        pl.semaphore_signal(across_sem, inc=1, device_id=device, device_id_type=MESH)

    for load in loads:
        load.wait()
    expand_bias(table, shear, xs, bias)
    ids_p, ids_q = window_ids(ids, row_of, lon_of, ms)
    same = ids_p == ids_q

    for own in owns:
        own.wait()
    arrive(halo)
    moved = dot(gather[...], field_in[...].reshape(TOK, D)).astype(BF)
    moved_grad = dot(gather[...], grad_in[...].reshape(TOK, D)).astype(BF)
    grad_qkv, grad_proj, local = window_grads(
        moved, moved_grad, same, gain[...].reshape(1, D), wqkv[...], wproj[...], bias, gs
    )

    pack_weights(grad_qkv, grad_proj, flat, w_out)
    rank = inside[1]
    pl.semaphore_wait(block_sem, FOUR - 1)
    pl.semaphore_wait(across_sem, 3)
    partner = (l + 1 - 2 * core, a)
    pair = []
    for k in range(4):
        copy = pltpu.make_async_remote_copy(
            src_ref=w_out.at[1 - core, 4 * k : 4 * k + 4],
            dst_ref=w_in.at[4 * k : 4 * k + 4],
            send_sem=pair_send.at[k],
            recv_sem=pair_recv.at[k],
            device_id=partner,
            device_id_type=MESH,
        )
        copy.start()
        pair.append(copy)

    tflat[...] = jnp.zeros_like(tflat)
    fold_bias(gs, shear, stacked, xs, tflat)
    for r in range(ACROSS):
        if r < 13:
            two = [tflat[:, 256 * r : 256 * r + 128], tflat[:, 256 * r + 128 : 256 * r + 256]]
            t_out[r] = jnp.concatenate(two, axis=0).astype(BF)
        else:
            t_out[r] = jnp.zeros((16, 128), BF)
    d1 = exchange(lambda r: t_out.at[r], t1, across, t1_send, t1_recv)
    t1[block] = t_out[block]

    arrive(pair)
    w_half[...] = (w_out[core].astype(F32) + w_in[...].astype(F32)).astype(BF)
    c1 = exchange(lambda r: w_half.at[r], w1, inside, w1_send, w1_recv)
    w1[rank] = w_half[rank]

    quads = dot_cols(gather[...], local()).astype(BF)
    quads_out[...] = quads.reshape(4, 3, 6, 2, D)
    back = []
    for s in range(1, 4):
        copy = pltpu.make_async_remote_copy(
            src_ref=quads_out.at[s],
            dst_ref=quads_in.at[s],
            send_sem=back_send.at[s],
            recv_sem=back_recv.at[s],
            device_id=far[s - 1],
            device_id_type=MESH,
        )
        copy.start()
        back.append(copy)
    quads_in[0] = quads_out[0]

    arrive(d1)
    mine = total_of(t1).astype(BF)
    t2_out[...] = mine
    t2[part] = mine
    d2 = exchange(lambda r: t2_out, t2, in_four, t2_send, t2_recv)

    arrive(c1)
    mine = total_of(w1).astype(BF)
    w2_out[...] = mine
    w2[block] = mine
    c2 = exchange(lambda r: w2_out, w2, across, w2_send, w2_recv)

    arrive(d2)
    t3[block] = total_of(t2).astype(BF)
    d3 = exchange(lambda r: t3.at[block], t3, across, t3_send, t3_recv)

    arrive(c2)
    w3[core, rank] = total_of(w2).astype(BF)
    c3 = exchange(lambda r: w3.at[core, rank], w3.at[core], inside, w3_send, w3_recv)

    arrive(back)
    out_quads[...] = quads_in[...]
    arrive(d3)
    out_table[...] = t3[...]
    c4 = []
    for k in range(INSIDE):
        if k:
            c3[k - 1].wait_recv()
        slot = lax.rem(rank + INSIDE - k, INSIDE)
        copy = pltpu.make_async_remote_copy(
            src_ref=w3.at[core, slot],
            dst_ref=w3.at[core, slot],
            send_sem=w4_send.at[k],
            recv_sem=w4_recv.at[k],
            device_id=partner,
            device_id_type=MESH,
        )
        copy.start()
        c4.append(copy)
    arrive(c4)
    out_flat[...] = w3[...]
    for copy in halo + back + pair + c1 + d1 + c2 + d2 + c3 + d3 + c4:
        copy.wait_send()


def finish(rows, quads, trows, grad_out, wqkv, gain, out_f, out_qkv, out_proj, out_gain, out_t, flat):
    finish_weights(rows, wqkv, gain, flat, out_qkv, out_proj, out_gain)
    finish_fields(quads, grad_out, out_f)
    finish_table(trows, out_t)


def body(fields, grad_out, mask_ids, ln_gain, qkv_weight, proj_weight, bias_table):
    consts = [jnp.asarray(v, BF) for v in token_tables()]
    fields = jnp.transpose(fields, (1, 2, 0, 3))
    grad_out = jnp.transpose(grad_out, (1, 2, 0, 3))
    vmem = pl.BlockSpec(memory_space=pltpu.VMEM)
    hbm = pl.BlockSpec(memory_space=pl.ANY)
    dma = pltpu.SemaphoreType.DMA
    scratch = [
        pltpu.VMEM((6, 2, 12), jnp.int32),
        pltpu.VMEM((D,), F32),
        pltpu.VMEM((D, 576), BF),
        pltpu.VMEM((D, D), BF),
        pltpu.VMEM((HEADS, 1, 3312), F32),
        pltpu.VMEM((TOK, TOK), BF),
        pltpu.VMEM((512, 384), BF),
        pltpu.VMEM((TOK, 16), BF),
        pltpu.VMEM((TOK, 128), BF),
        pltpu.VMEM((4, 3, 6, 2, D), BF),
        pltpu.VMEM((4, 3, 6, 2, D), BF),
        pltpu.VMEM((4, 72, 128), F32),
        pltpu.VMEM((HEADS, TOK, TOK), F32),
        pltpu.VMEM((HEADS, TOK, TOK), F32),
        pltpu.VMEM((LON, 72, TOK), F32),
        pltpu.VMEM((16, 128), F32),
        pltpu.VMEM((8, 3328), F32),
        pltpu.VMEM((4, 3, 6, 2, D), BF),
        pltpu.VMEM((4, 3, 6, 2, D), BF),
        pltpu.VMEM((1152, 128), F32),
        pltpu.VMEM((2, INSIDE, ROWS, 128), BF),
        pltpu.VMEM((INSIDE, ROWS, 128), BF),
        pltpu.VMEM((INSIDE, ROWS, 128), BF),
        pltpu.VMEM((INSIDE, ROWS, 128), BF),
        pltpu.VMEM((ROWS, 128), BF),
        pltpu.VMEM((ACROSS, ROWS, 128), BF),
        pltpu.VMEM((2, INSIDE, ROWS, 128), BF),
        pltpu.VMEM((ACROSS, 16, 128), BF),
        pltpu.VMEM((ACROSS, 16, 128), BF),
        pltpu.VMEM((16, 128), BF),
        pltpu.VMEM((FOUR, 16, 128), BF),
        pltpu.VMEM((ACROSS, 16, 128), BF),
        pltpu.SemaphoreType.REGULAR,
        pltpu.SemaphoreType.REGULAR,
        dma((9,)),
        dma((2,)),
        dma((8,)),
        dma((8,)),
        dma((4,)),
        dma((4,)),
        dma((4,)),
        dma((4,)),
        dma((INSIDE,)),
        dma((INSIDE,)),
        dma((ACROSS,)),
        dma((ACROSS,)),
        dma((INSIDE,)),
        dma((INSIDE,)),
        dma((INSIDE,)),
        dma((INSIDE,)),
        dma((ACROSS,)),
        dma((ACROSS,)),
        dma((FOUR,)),
        dma((FOUR,)),
        dma((ACROSS,)),
        dma((ACROSS,)),
    ]
    rows, quads, trows = pl.pallas_call(
        kernel,
        out_shape=(
            jax.ShapeDtypeStruct((2, INSIDE, ROWS, 128), BF),
            jax.ShapeDtypeStruct((4, 3, 6, 2, D), BF),
            jax.ShapeDtypeStruct((ACROSS, 16, 128), BF),
        ),
        in_specs=[hbm] * 11,
        out_specs=(vmem, vmem, vmem),
        scratch_shapes=scratch,
        compiler_params=pltpu.CompilerParams(
            collective_id=0, has_side_effects=True, vmem_limit_bytes=VMEM_LIMIT
        ),
    )(
        fields, grad_out, jnp.transpose(mask_ids, (1, 0, 2)), ln_gain, qkv_weight, proj_weight,
        bias_table.reshape(HEADS, 1, 3312), *consts,
    )
    out_f, out_qkv, out_proj, out_gain, out_t = pl.pallas_call(
        finish,
        out_shape=(
            jax.ShapeDtypeStruct((6, 12, 2, D), BF),
            jax.ShapeDtypeStruct((D, 576), F32),
            jax.ShapeDtypeStruct((D, D), F32),
            jax.ShapeDtypeStruct((D,), F32),
            jax.ShapeDtypeStruct((HEADS, 1, 3312), F32),
        ),
        in_specs=[vmem] * 6,
        out_specs=(vmem,) * 5,
        scratch_shapes=[pltpu.VMEM((1152, 128), F32)],
        compiler_params=pltpu.CompilerParams(vmem_limit_bytes=VMEM_LIMIT),
    )(rows, quads, trows, grad_out, qkv_weight, ln_gain)
    out_f = jnp.transpose(out_f, (2, 0, 1, 3))
    return out_f, out_qkv, out_proj, out_gain, out_t.reshape(1, 1, HEADS, 3312)


def solution(mesh):
    placed = (
        P(None, "lat", "lon", None),
        P(None, "lat", "lon", None),
        P(None, "lat", "lon"),
        P(),
        P(),
        P(),
        P("lat", None, None, None),
    )
    return jax.shard_map(
        body,
        mesh=mesh,
        in_specs=placed,
        out_specs=(P(None, "lat", "lon", None), P(), P(), P(), P("lat", None, None, None)),
        check_vma=False,
    )
```

```python
import functools

import jax
import jax.numpy as jnp
import numpy as np
from jax import lax
from jax.experimental import pallas as pl
from jax.experimental.pallas import tpu as pltpu
from jax.sharding import PartitionSpec as P

D = 192
HEADS = 6
LON = 12
CELLS = 12
TOK = 144
SPAN = 23 * CELLS
SEG = 138
EPS = 1e-05
MESH = pl.DeviceIdType.MESH
BF = jnp.bfloat16
F32 = jnp.float32

INSIDE, ACROSS, FOUR = 16, 16, 4
ROWS = 1152 // (2 * INSIDE)
VMEM_LIMIT = 60 * 1024 * 1024


def token_tables():
    gather = np.zeros((TOK, TOK), np.float32)
    for o in range(12):
        for z in range(2):
            for a in range(6):
                s = (a >= 3) * 2 + (o >= 6)
                gather[o * 12 + z * 6 + a, ((s * 3 + a % 3) * 6 + o % 6) * 2 + (z + 1) % 2] = 1
    shear = np.zeros((512, 384), np.float32)
    for zq in range(2):
        for aq in range(6):
            for r in range(23):
                shear[zq * 256 + aq * 23 + r, r * 12 + zq * 6 + aq] = 1
    row_of = np.zeros((TOK, 16), np.float32)
    lon_of = np.zeros((TOK, 128), np.float32)
    for t in range(TOK):
        row_of[t, t % 12] = 1
        lon_of[t, t // 12] = 1
    return gather, shear, row_of, lon_of


def dot(a, b):
    return lax.dot_general(a, b, (((1,), (0,)), ((), ())), preferred_element_type=F32)


def dot_rows(a, b):
    return lax.dot_general(a, b, (((1,), (1,)), ((), ())), preferred_element_type=F32)


def dot_cols(a, b):
    return lax.dot_general(a, b, (((0,), (0,)), ((), ())), preferred_element_type=F32)


def split(v):
    hi = v.astype(BF)
    return hi, (v - hi.astype(F32)).astype(BF)


def expand_bias(table, shear, xs, bias):
    for zp in range(2):
        for zq in range(2):
            for ap in range(6):
                start = ((zp * 2 + zq) * 6 + ap) * SEG
                rows = pl.ds(zp * 6 + ap, HEADS, stride=CELLS)
                part = table[:, 0, start : start + SEG]
                rest = jnp.concatenate([part[:, 128:], jnp.zeros((HEADS, 256 - SEG), F32)], axis=1)
                xs[2 * zq, rows, :] = part[:, 0:128]
                xs[2 * zq + 1, rows, :] = rest
    hi, lo = split(jnp.concatenate([xs[k] for k in range(4)], axis=1))
    sheared = dot(hi, shear[...]) + dot(lo, shear[...])
    for op in range(LON):
        window = sheared[:, (11 - op) * 12 : (11 - op) * 12 + TOK]
        for h in range(HEADS):
            bias[h, op * 12 : (op + 1) * 12, :] = window[h * 12 : (h + 1) * 12]


def fold_bias(gs, shear, stacked, xs, flat):
    for op in range(LON):
        for h in range(HEADS):
            stacked[op, h * 12 : (h + 1) * 12, :] = gs[h, op * 12 : (op + 1) * 12, :]
    total = None
    for op in range(LON):
        left = (11 - op) * 12
        parts = [stacked[op]]
        if left:
            parts.insert(0, jnp.zeros((72, left), F32))
        if SPAN - left - TOK:
            parts.append(jnp.zeros((72, SPAN - left - TOK), F32))
        piece = jnp.concatenate(parts, axis=1) if len(parts) > 1 else parts[0]
        total = piece if total is None else total + piece
    total = jnp.concatenate([total, jnp.zeros((72, 384 - SPAN), F32)], axis=1)
    hi, lo = split(total)
    spread = dot_rows(hi, shear[...]) + dot_rows(lo, shear[...])
    for k in range(4):
        xs[k] = spread[:, 128 * k : 128 * k + 128]
    for zp in range(2):
        for zq in range(2):
            for ap in range(6):
                start = ((zp * 2 + zq) * 6 + ap) * SEG
                rows = pl.ds(zp * 6 + ap, HEADS, stride=CELLS)
                flat[0:HEADS, start : start + 128] = xs[2 * zq, rows, :]
                flat[0:HEADS, start + 128 : start + SEG] = xs[2 * zq + 1, rows, :][:, 0 : SEG - 128]


def window_ids(ids, row_of, lon_of, ms):
    ms[...] = jnp.zeros_like(ms)
    for a in range(6):
        ms[a : a + 1, 0:12] = ids[a, 0:1].astype(F32)
        ms[a + 6 : a + 7, 0:12] = ids[a, 1:2].astype(F32)
    m = ms[...].astype(BF)
    column = jnp.sum(dot(row_of[...], m) * lon_of[...].astype(F32), axis=1, keepdims=True)
    spread = dot_cols(m, row_of[...].astype(F32).T.astype(BF))
    row = jnp.sum(spread * lon_of[...].astype(F32).T, axis=0, keepdims=True)
    return column, row


def window_grads(x, g, same, gain, wqkv, wproj, bias, gs_out):
    x = x.astype(F32)
    centred = x - jnp.mean(x, axis=-1, keepdims=True)
    inv_std = lax.rsqrt(jnp.mean(centred * centred, axis=-1, keepdims=True) + EPS)
    normed = centred * inv_std
    hidden = (normed * gain).astype(BF)
    projected = dot(hidden, wqkv)
    scaling = 32 ** (-0.5)
    query = (projected[:, :D] * scaling).astype(BF)
    key = projected[:, D : 2 * D].astype(BF)
    value = projected[:, 2 * D :].astype(BF)
    grad_att = dot_rows(g, wproj).astype(BF)
    lane = lax.broadcasted_iota(jnp.int32, (TOK, D), 1) // 32
    zero = jnp.zeros((TOK, D), BF)
    heads = range(HEADS)

    def by_head(v):
        return [jnp.where(lane == h, v, zero) for h in heads]

    def stack(v):
        return jnp.concatenate(v, axis=0)

    def unstack(v):
        return [v[h * TOK : (h + 1) * TOK] for h in heads]

    def over_heads(left, right):
        total = dot(left[0], right[0])
        for h in range(1, HEADS):
            total = total + dot(left[h], right[h])
        return total

    queries, grads = stack(by_head(query)), stack(by_head(grad_att))
    scores = unstack(dot_rows(queries, key))
    grad_prob = unstack(dot_rows(grads, value))
    scores = [jnp.where(same, scores[h] + bias[h], -1000000000.0) for h in heads]
    raised = [jnp.exp(v - jnp.max(v, axis=-1, keepdims=True)) for v in scores]
    prob = [v * (1.0 / jnp.sum(v, axis=-1, keepdims=True)) for v in raised]
    prob_bf = [v.astype(BF) for v in prob]
    weighted = [prob[h] * grad_prob[h] for h in heads]
    gs = [w - p * jnp.sum(w, axis=-1, keepdims=True) for w, p in zip(weighted, prob)]
    for h in heads:
        gs_out[h] = gs[h]
    gs = [v.astype(BF) for v in gs]
    attended = over_heads(prob_bf, by_head(value))
    dv = dot_cols(stack(prob_bf), grads)
    dq = over_heads(gs, by_head(key))
    dk = dot_cols(stack(gs), queries)
    joint = jnp.concatenate(
        [(dq * scaling).astype(BF), dk.astype(BF), dv.astype(BF)], axis=1
    )
    grad_qkv = dot_cols(hidden, joint)
    grad_proj = dot_cols(attended.astype(BF), g)

    def local():
        grad_hidden = dot_rows(joint, wqkv)
        scaled = grad_hidden * gain
        return (
            inv_std
            * (
                scaled
                - jnp.mean(scaled, axis=-1, keepdims=True)
                - normed * jnp.mean(scaled * normed, axis=-1, keepdims=True)
            )
        ).astype(BF)

    return grad_qkv, grad_proj, local


def pack_weights(grad_qkv, grad_proj, flat, out):
    for c in range(4):
        flat[c * 192 : (c + 1) * 192, :] = grad_qkv[:, c * 128 : (c + 1) * 128]
    flat[768:960, :] = jnp.concatenate([grad_qkv[:, 512:576], grad_proj[:, 128:192]], axis=1)
    flat[960:1152, :] = grad_proj[:, 0:128]
    for r in range(2 * INSIDE):
        out[r // INSIDE, r % INSIDE] = flat[ROWS * r : ROWS * (r + 1), :].astype(BF)


def finish_weights(rows, wqkv, gain, flat, out_qkv, out_proj, out_gain):
    for r in range(2 * INSIDE):
        flat[ROWS * r : ROWS * (r + 1), :] = rows[r // INSIDE, r % INSIDE].astype(F32)
    for c in range(4):
        out_qkv[:, c * 128 : (c + 1) * 128] = flat[c * 192 : (c + 1) * 192, :]
    last = flat[768:960, :]
    out_qkv[:, 512:576] = last[:, 0:64]
    out_proj[:, 128:192] = last[:, 64:128]
    out_proj[:, 0:128] = flat[960:1152, :]
    products = out_qkv[...] * wqkv[...].astype(F32)
    hi, lo = split(products)
    ones = jnp.ones((8, 576), BF)
    row = (dot_rows(ones, hi) + dot_rows(ones, lo))[0:1]
    out_gain[...] = (row / gain[...].reshape(1, D)).reshape(D)


def finish_fields(quads, grad_out, out):
    for s in range(4):
        rows = slice(0, 3) if s >= 2 else slice(3, 6)
        cols = slice(0, 6) if s % 2 else slice(6, 12)
        out[rows, cols] = (grad_out[rows, cols].astype(F32) + quads[s].astype(F32)).astype(BF)


def finish_table(rows, out):
    for k in range(26):
        width = min(128, 3312 - 128 * k)
        block = rows[k // 2].astype(F32)[8 * (k % 2) : 8 * (k % 2) + 8]
        for h in range(HEADS):
            out[h, :, 128 * k : 128 * k + width] = block[h : h + 1, 0:width]


def exchange(src_of, recv, group, send_sem, recv_sem):
    size, rank, device_of = group
    copies = []
    for k in range(1, size):
        peer = lax.rem(rank + k, size)
        copy = pltpu.make_async_remote_copy(
            src_ref=src_of(peer),
            dst_ref=recv.at[rank],
            send_sem=send_sem,
            recv_sem=recv_sem.at[k] if len(recv_sem.shape) else recv_sem,
            device_id=device_of(peer),
            device_id_type=MESH,
        )
        copy.start()
        copies.append(copy)
    return copies


def wait_bytes(ref, sem):
    pltpu.make_async_copy(ref, ref, sem).wait()


def arrive(copies):
    for copy in copies:
        copy.wait_recv()


def total_of(recv):
    total = recv[0].astype(F32)
    for k in range(1, recv.shape[0]):
        total = total + recv[k].astype(F32)
    return total


def kernel(
    fields, grad_out, ids_hbm, gain_hbm, wqkv_hbm, wproj_hbm, table_hbm,
    gather_hbm, shear_hbm, row_hbm, lon_hbm,
    out_flat, out_quads, out_table,
    ids, gain, wqkv, wproj, table, gather, shear, row_of, lon_of,
    field_in, grad_in, xs, bias, gs, stacked, ms, tflat, quads_out, quads_in,
    flat, w_out, w_in, w_half, w1, w2_out, w2, w3, t_out, t1, t2_out, t2, t3,
    block_sem, across_sem, load_sem, own_sem, halo_send, halo_recv, back_send, back_recv,
    pair_send, pair_recv, w1_send, w1_recv, w2_send, w2_recv, w3_send, w3_recv, w4_send, w4_recv,
    t1_send, t1_recv, t2_send, t2_recv, t3_send, t3_recv,
):
    l, a = lax.axis_index("lon"), lax.axis_index("lat")
    part, block = lax.rem(l, FOUR), l // FOUR
    core, side = lax.rem(part, 2), part // 2
    near_l, far_l = lax.rem(l + 63, 64), lax.rem(l + 1, 64)
    near_a, far_a = lax.rem(a + 7, 8), lax.rem(a + 1, 8)

    inside = (INSIDE, a * 2 + side, lambda r: (block * FOUR + lax.rem(r, 2) * 2 + core, r // 2))
    across = (ACROSS, block, lambda r: (r * FOUR + part, a))
    in_four = (FOUR, part, lambda r: (block * FOUR + r, a))
    barrier = pltpu.get_barrier_semaphore()
    near = ((near_l, a), (l, near_a), (near_l, near_a))
    far = ((far_l, a), (l, far_a), (far_l, far_a))
    beside = [(near_l, a), (far_l, a), near[2], far[2]]
    column = [(l, lax.rem(a + k, 8)) for k in range(1, 8)]
    four = [(block * FOUR + lax.rem(part + k, FOUR), a) for k in range(1, FOUR)]
    high, low = block // 4, lax.rem(block, 4)
    lows = [((high * 4 + lax.rem(low + k, 4)) * FOUR + part, a) for k in range(1, 4)]
    highs = [((lax.rem(high + k, 4) * 4 + low) * FOUR + part, a) for k in range(1, 4)]
    entry = highs + lows + column + beside + four
    for device in entry:
        pl.semaphore_signal(barrier, inc=1, device_id=device, device_id_type=MESH)
    loads = []
    pairs = (
        (table_hbm, table), (shear_hbm, shear), (ids_hbm, ids), (row_hbm, row_of), (lon_hbm, lon_of),
        (gather_hbm, gather), (gain_hbm, gain), (wqkv_hbm, wqkv), (wproj_hbm, wproj),
    )
    for k, (src, dst) in enumerate(pairs):
        load = pltpu.make_async_copy(src, dst, load_sem.at[k])
        load.start()
        loads.append(load)
    owns = []
    for k, (src, dst) in enumerate(((fields, field_in), (grad_out, grad_in))):
        own = pltpu.make_async_copy(src.at[3:6, 6:12], dst.at[0], own_sem.at[k])
        own.start()
        owns.append(own)
    pl.semaphore_wait(barrier, len(entry))

    halo = []
    for s in range(1, 4):
        rows = slice(0, 3) if s >= 2 else slice(3, 6)
        cols = slice(0, 6) if s % 2 else slice(6, 12)
        for k, (src, dst) in enumerate(((fields, field_in), (grad_out, grad_in))):
            copy = pltpu.make_async_remote_copy(
                src_ref=src.at[rows, cols],
                dst_ref=dst.at[s],
                send_sem=halo_send.at[2 * s + k],
                recv_sem=halo_recv.at[2 * s + k],
                device_id=near[s - 1],
                device_id_type=MESH,
            )
            copy.start()
            halo.append(copy)

    for device in four:
        pl.semaphore_signal(block_sem, inc=1, device_id=device, device_id_type=MESH)
    for device in highs:
        pl.semaphore_signal(across_sem, inc=1, device_id=device, device_id_type=MESH)

    for load in loads:
        load.wait()
    expand_bias(table, shear, xs, bias)
    ids_p, ids_q = window_ids(ids, row_of, lon_of, ms)
    same = ids_p == ids_q

    for own in owns:
        own.wait()
    arrive(halo)
    moved = dot(gather[...], field_in[...].reshape(TOK, D)).astype(BF)
    moved_grad = dot(gather[...], grad_in[...].reshape(TOK, D)).astype(BF)
    grad_qkv, grad_proj, local = window_grads(
        moved, moved_grad, same, gain[...].reshape(1, D), wqkv[...], wproj[...], bias, gs
    )

    pack_weights(grad_qkv, grad_proj, flat, w_out)
    rank = inside[1]
    pl.semaphore_wait(block_sem, FOUR - 1)
    pl.semaphore_wait(across_sem, 3)
    partner = (l + 1 - 2 * core, a)
    pltpu.make_async_remote_copy(
        src_ref=w_out.at[1 - core],
        dst_ref=w_in,
        send_sem=pair_send,
        recv_sem=pair_recv,
        device_id=partner,
        device_id_type=MESH,
    ).start()

    quads = dot_cols(gather[...], local()).astype(BF)
    quads_out[...] = quads.reshape(4, 3, 6, 2, D)
    back = []
    for s in range(1, 4):
        copy = pltpu.make_async_remote_copy(
            src_ref=quads_out.at[s],
            dst_ref=quads_in.at[s],
            send_sem=back_send.at[s],
            recv_sem=back_recv.at[s],
            device_id=far[s - 1],
            device_id_type=MESH,
        )
        copy.start()
        back.append(copy)
    quads_in[0] = quads_out[0]

    wait_bytes(w_in, pair_recv)
    w_half[...] = (w_out[core].astype(F32) + w_in[...].astype(F32)).astype(BF)
    exchange(lambda r: w_half.at[r], w1, inside, w1_send, w1_recv)
    w1[rank] = w_half[rank]

    tflat[...] = jnp.zeros_like(tflat)
    fold_bias(gs, shear, stacked, xs, tflat)
    for r in range(ACROSS):
        if r < 13:
            two = [tflat[:, 256 * r : 256 * r + 128], tflat[:, 256 * r + 128 : 256 * r + 256]]
            t_out[r] = jnp.concatenate(two, axis=0).astype(BF)
        else:
            t_out[r] = jnp.zeros((16, 128), BF)
    exchange(lambda r: t_out.at[r], t1, across, t1_send, t1_recv)
    t1[block] = t_out[block]
    for copy in halo:
        copy.wait_send()
    wait_bytes(w_in, pair_send)

    wait_bytes(w1.at[1:], w1_recv)
    mine = total_of(w1).astype(BF)
    w2_out[...] = mine
    w2[block] = mine
    exchange(lambda r: w2_out, w2, across, w2_send, w2_recv)

    wait_bytes(t1.at[1:], t1_recv)
    mine = total_of(t1).astype(BF)
    t2_out[...] = mine
    t2[part] = mine
    exchange(lambda r: t2_out, t2, in_four, t2_send, t2_recv)
    wait_bytes(w1.at[1:], w1_send)
    wait_bytes(t1.at[1:], t1_send)
    arrive(back)
    out_quads[...] = quads_in[...]

    wait_bytes(t2.at[1:], t2_recv)
    t3[block] = total_of(t2).astype(BF)
    exchange(lambda r: t3.at[block], t3, across, t3_send, t3_recv)

    wait_bytes(w2.at[1:], w2_recv)
    w3[core, rank] = total_of(w2).astype(BF)
    c3 = exchange(lambda r: w3.at[core, rank], w3.at[core], inside, w3_send, w3_recv)
    for copy in back:
        copy.wait_send()
    wait_bytes(w2.at[1:], w2_send)
    wait_bytes(t2.at[1:], t2_send)

    for k in range(INSIDE):
        if k:
            c3[k - 1].wait_recv()
        slot = lax.rem(rank + INSIDE - k, INSIDE)
        pltpu.make_async_remote_copy(
            src_ref=w3.at[core, slot],
            dst_ref=w3.at[core, slot],
            send_sem=w4_send,
            recv_sem=w4_recv,
            device_id=partner,
            device_id_type=MESH,
        ).start()
    wait_bytes(t3.at[1:], t3_recv)
    out_table[...] = t3[...]
    wait_bytes(t3.at[1:], t3_send)
    wait_bytes(w1.at[1:], w3_send)
    wait_bytes(w1, w4_recv)
    out_flat[...] = w3[...]
    wait_bytes(w1, w4_send)


def finish(rows, quads, trows, grad_out, wqkv, gain, out_f, out_qkv, out_proj, out_gain, out_t, flat):
    finish_weights(rows, wqkv, gain, flat, out_qkv, out_proj, out_gain)
    finish_fields(quads, grad_out, out_f)
    finish_table(trows, out_t)


def body(fields, grad_out, mask_ids, ln_gain, qkv_weight, proj_weight, bias_table):
    consts = [jnp.asarray(v, BF) for v in token_tables()]
    fields = jnp.transpose(fields, (1, 2, 0, 3))
    grad_out = jnp.transpose(grad_out, (1, 2, 0, 3))
    vmem = pl.BlockSpec(memory_space=pltpu.VMEM)
    hbm = pl.BlockSpec(memory_space=pl.ANY)
    dma = pltpu.SemaphoreType.DMA
    scratch = [
        pltpu.VMEM((6, 2, 12), jnp.int32),
        pltpu.VMEM((D,), F32),
        pltpu.VMEM((D, 576), BF),
        pltpu.VMEM((D, D), BF),
        pltpu.VMEM((HEADS, 1, 3312), F32),
        pltpu.VMEM((TOK, TOK), BF),
        pltpu.VMEM((512, 384), BF),
        pltpu.VMEM((TOK, 16), BF),
        pltpu.VMEM((TOK, 128), BF),
        pltpu.VMEM((4, 3, 6, 2, D), BF),
        pltpu.VMEM((4, 3, 6, 2, D), BF),
        pltpu.VMEM((4, 72, 128), F32),
        pltpu.VMEM((HEADS, TOK, TOK), F32),
        pltpu.VMEM((HEADS, TOK, TOK), F32),
        pltpu.VMEM((LON, 72, TOK), F32),
        pltpu.VMEM((16, 128), F32),
        pltpu.VMEM((8, 3328), F32),
        pltpu.VMEM((4, 3, 6, 2, D), BF),
        pltpu.VMEM((4, 3, 6, 2, D), BF),
        pltpu.VMEM((1152, 128), F32),
        pltpu.VMEM((2, INSIDE, ROWS, 128), BF),
        pltpu.VMEM((INSIDE, ROWS, 128), BF),
        pltpu.VMEM((INSIDE, ROWS, 128), BF),
        pltpu.VMEM((INSIDE, ROWS, 128), BF),
        pltpu.VMEM((ROWS, 128), BF),
        pltpu.VMEM((ACROSS, ROWS, 128), BF),
        pltpu.VMEM((2, INSIDE, ROWS, 128), BF),
        pltpu.VMEM((ACROSS, 16, 128), BF),
        pltpu.VMEM((ACROSS, 16, 128), BF),
        pltpu.VMEM((16, 128), BF),
        pltpu.VMEM((FOUR, 16, 128), BF),
        pltpu.VMEM((ACROSS, 16, 128), BF),
        pltpu.SemaphoreType.REGULAR,
        pltpu.SemaphoreType.REGULAR,
        dma((9,)),
        dma((2,)),
        dma((8,)),
        dma((8,)),
        dma((4,)),
        dma((4,)),
        *([dma] * 7),
        dma((INSIDE,)),
        *([dma] * 8),
    ]
    rows, quads, trows = pl.pallas_call(
        kernel,
        out_shape=(
            jax.ShapeDtypeStruct((2, INSIDE, ROWS, 128), BF),
            jax.ShapeDtypeStruct((4, 3, 6, 2, D), BF),
            jax.ShapeDtypeStruct((ACROSS, 16, 128), BF),
        ),
        in_specs=[hbm] * 11,
        out_specs=(vmem, vmem, vmem),
        scratch_shapes=scratch,
        compiler_params=pltpu.CompilerParams(
            collective_id=0, has_side_effects=True, vmem_limit_bytes=VMEM_LIMIT
        ),
    )(
        fields, grad_out, jnp.transpose(mask_ids, (1, 0, 2)), ln_gain, qkv_weight, proj_weight,
        bias_table.reshape(HEADS, 1, 3312), *consts,
    )
    out_f, out_qkv, out_proj, out_gain, out_t = pl.pallas_call(
        finish,
        out_shape=(
            jax.ShapeDtypeStruct((6, 12, 2, D), BF),
            jax.ShapeDtypeStruct((D, 576), F32),
            jax.ShapeDtypeStruct((D, D), F32),
            jax.ShapeDtypeStruct((D,), F32),
            jax.ShapeDtypeStruct((HEADS, 1, 3312), F32),
        ),
        in_specs=[vmem] * 6,
        out_specs=(vmem,) * 5,
        scratch_shapes=[pltpu.VMEM((1152, 128), F32)],
        compiler_params=pltpu.CompilerParams(vmem_limit_bytes=VMEM_LIMIT),
    )(rows, quads, trows, grad_out, qkv_weight, ln_gain)
    out_f = jnp.transpose(out_f, (2, 0, 1, 3))
    return out_f, out_qkv, out_proj, out_gain, out_t.reshape(1, 1, HEADS, 3312)


def solution(mesh):
    placed = (
        P(None, "lat", "lon", None),
        P(None, "lat", "lon", None),
        P(None, "lat", "lon"),
        P(),
        P(),
        P(),
        P("lat", None, None, None),
    )
    return jax.shard_map(
        body,
        mesh=mesh,
        in_specs=placed,
        out_specs=(P(None, "lat", "lon", None), P(), P(), P(), P("lat", None, None, None)),
        check_vma=False,
    )
```

```python
import functools

import jax
import jax.numpy as jnp
import numpy as np
from jax import lax
from jax.experimental import pallas as pl
from jax.experimental.pallas import tpu as pltpu
from jax.sharding import PartitionSpec as P

D = 192
HEADS = 6
LON = 12
CELLS = 12
TOK = 144
SPAN = 23 * CELLS
SEG = 138
EPS = 1e-05
MESH = pl.DeviceIdType.MESH
BF = jnp.bfloat16
F32 = jnp.float32

INSIDE, ACROSS, FOUR = 16, 16, 4
ROWS = 1152 // (2 * INSIDE)
VMEM_LIMIT = 60 * 1024 * 1024


def token_tables():
    gather = np.zeros((TOK, TOK), np.float32)
    for o in range(12):
        for z in range(2):
            for a in range(6):
                s = (a >= 3) * 2 + (o >= 6)
                gather[o * 12 + z * 6 + a, ((s * 3 + a % 3) * 6 + o % 6) * 2 + (z + 1) % 2] = 1
    shear = np.zeros((512, 384), np.float32)
    for zq in range(2):
        for aq in range(6):
            for r in range(23):
                shear[zq * 256 + aq * 23 + r, r * 12 + zq * 6 + aq] = 1
    row_of = np.zeros((TOK, 16), np.float32)
    lon_of = np.zeros((TOK, 128), np.float32)
    for t in range(TOK):
        row_of[t, t % 12] = 1
        lon_of[t, t // 12] = 1
    return gather, shear, row_of, lon_of


def dot(a, b):
    return lax.dot_general(a, b, (((1,), (0,)), ((), ())), preferred_element_type=F32)


def dot_rows(a, b):
    return lax.dot_general(a, b, (((1,), (1,)), ((), ())), preferred_element_type=F32)


def dot_cols(a, b):
    return lax.dot_general(a, b, (((0,), (0,)), ((), ())), preferred_element_type=F32)


def split(v):
    hi = v.astype(BF)
    return hi, (v - hi.astype(F32)).astype(BF)


def expand_bias(table, shear, xs, bias):
    for zp in range(2):
        for zq in range(2):
            for ap in range(6):
                start = ((zp * 2 + zq) * 6 + ap) * SEG
                rows = pl.ds(zp * 6 + ap, HEADS, stride=CELLS)
                part = table[:, 0, start : start + SEG]
                rest = jnp.concatenate([part[:, 128:], jnp.zeros((HEADS, 256 - SEG), F32)], axis=1)
                xs[2 * zq, rows, :] = part[:, 0:128]
                xs[2 * zq + 1, rows, :] = rest
    hi, lo = split(jnp.concatenate([xs[k] for k in range(4)], axis=1))
    sheared = dot(hi, shear[...]) + dot(lo, shear[...])
    for op in range(LON):
        window = sheared[:, (11 - op) * 12 : (11 - op) * 12 + TOK]
        for h in range(HEADS):
            bias[h, op * 12 : (op + 1) * 12, :] = window[h * 12 : (h + 1) * 12]


def fold_bias(gs, shear, stacked, xs, flat):
    for op in range(LON):
        for h in range(HEADS):
            stacked[op, h * 12 : (h + 1) * 12, :] = gs[h, op * 12 : (op + 1) * 12, :]
    total = None
    for op in range(LON):
        left = (11 - op) * 12
        parts = [stacked[op]]
        if left:
            parts.insert(0, jnp.zeros((72, left), F32))
        if SPAN - left - TOK:
            parts.append(jnp.zeros((72, SPAN - left - TOK), F32))
        piece = jnp.concatenate(parts, axis=1) if len(parts) > 1 else parts[0]
        total = piece if total is None else total + piece
    total = jnp.concatenate([total, jnp.zeros((72, 384 - SPAN), F32)], axis=1)
    hi, lo = split(total)
    spread = dot_rows(hi, shear[...]) + dot_rows(lo, shear[...])
    for k in range(4):
        xs[k] = spread[:, 128 * k : 128 * k + 128]
    for zp in range(2):
        for zq in range(2):
            for ap in range(6):
                start = ((zp * 2 + zq) * 6 + ap) * SEG
                rows = pl.ds(zp * 6 + ap, HEADS, stride=CELLS)
                flat[0:HEADS, start : start + 128] = xs[2 * zq, rows, :]
                flat[0:HEADS, start + 128 : start + SEG] = xs[2 * zq + 1, rows, :][:, 0 : SEG - 128]


def window_ids(ids, row_of, lon_of, ms):
    ms[...] = jnp.zeros_like(ms)
    for a in range(6):
        ms[a : a + 1, 0:12] = ids[a, 0:1].astype(F32)
        ms[a + 6 : a + 7, 0:12] = ids[a, 1:2].astype(F32)
    m = ms[...].astype(BF)
    column = jnp.sum(dot(row_of[...], m) * lon_of[...].astype(F32), axis=1, keepdims=True)
    spread = dot_cols(m, row_of[...].astype(F32).T.astype(BF))
    row = jnp.sum(spread * lon_of[...].astype(F32).T, axis=0, keepdims=True)
    return column, row


def window_grads(x, g, gain, wqkv, wproj, bias, gs_out):
    x = x.astype(F32)
    centred = x - jnp.mean(x, axis=-1, keepdims=True)
    inv_std = lax.rsqrt(jnp.mean(centred * centred, axis=-1, keepdims=True) + EPS)
    normed = centred * inv_std
    hidden = (normed * gain).astype(BF)
    projected = dot(hidden, wqkv)
    scaling = 32 ** (-0.5)
    query = (projected[:, :D] * scaling).astype(BF)
    key = projected[:, D : 2 * D].astype(BF)
    value = projected[:, 2 * D :].astype(BF)
    grad_att = dot_rows(g, wproj).astype(BF)
    lane = lax.broadcasted_iota(jnp.int32, (TOK, D), 1) // 32
    zero = jnp.zeros((TOK, D), BF)
    heads = range(HEADS)

    def by_head(v):
        return [jnp.where(lane == h, v, zero) for h in heads]

    def stack(v):
        return jnp.concatenate(v, axis=0)

    def unstack(v):
        return [v[h * TOK : (h + 1) * TOK] for h in heads]

    def over_heads(left, right):
        total = dot(left[0], right[0])
        for h in range(1, HEADS):
            total = total + dot(left[h], right[h])
        return total

    queries, grads = stack(by_head(query)), stack(by_head(grad_att))
    scores = unstack(dot_rows(queries, key))
    grad_prob = unstack(dot_rows(grads, value))
    scores = [scores[h] + bias[h] for h in heads]
    raised = [jnp.exp(v - jnp.max(v, axis=-1, keepdims=True)) for v in scores]
    prob = [v * (1.0 / jnp.sum(v, axis=-1, keepdims=True)) for v in raised]
    prob_bf = [v.astype(BF) for v in prob]
    weighted = [prob[h] * grad_prob[h] for h in heads]
    gs = [w - p * jnp.sum(w, axis=-1, keepdims=True) for w, p in zip(weighted, prob)]
    for h in heads:
        gs_out[h] = gs[h]
    gs = [v.astype(BF) for v in gs]
    attended = over_heads(prob_bf, by_head(value))
    dv = dot_cols(stack(prob_bf), grads)
    dq = over_heads(gs, by_head(key))
    dk = dot_cols(stack(gs), queries)
    joint = jnp.concatenate(
        [(dq * scaling).astype(BF), dk.astype(BF), dv.astype(BF)], axis=1
    )
    grad_qkv = dot_cols(hidden, joint)
    grad_proj = dot_cols(attended.astype(BF), g)

    def local():
        grad_hidden = dot_rows(joint, wqkv)
        scaled = grad_hidden * gain
        return (
            inv_std
            * (
                scaled
                - jnp.mean(scaled, axis=-1, keepdims=True)
                - normed * jnp.mean(scaled * normed, axis=-1, keepdims=True)
            )
        ).astype(BF)

    return grad_qkv, grad_proj, local


def pack_weights(grad_qkv, grad_proj, flat, out):
    for c in range(4):
        flat[c * 192 : (c + 1) * 192, :] = grad_qkv[:, c * 128 : (c + 1) * 128]
    flat[768:960, :] = jnp.concatenate([grad_qkv[:, 512:576], grad_proj[:, 128:192]], axis=1)
    flat[960:1152, :] = grad_proj[:, 0:128]
    for r in range(2 * INSIDE):
        out[r // INSIDE, r % INSIDE] = flat[ROWS * r : ROWS * (r + 1), :].astype(BF)


def finish_weights(rows, wqkv, gain, flat, out_qkv, out_proj, out_gain):
    for r in range(2 * INSIDE):
        flat[ROWS * r : ROWS * (r + 1), :] = rows[r // INSIDE, r % INSIDE].astype(F32)
    for c in range(4):
        out_qkv[:, c * 128 : (c + 1) * 128] = flat[c * 192 : (c + 1) * 192, :]
    last = flat[768:960, :]
    out_qkv[:, 512:576] = last[:, 0:64]
    out_proj[:, 128:192] = last[:, 64:128]
    out_proj[:, 0:128] = flat[960:1152, :]
    products = out_qkv[...] * wqkv[...].astype(F32)
    hi, lo = split(products)
    ones = jnp.ones((8, 576), BF)
    row = (dot_rows(ones, hi) + dot_rows(ones, lo))[0:1]
    out_gain[...] = (row / gain[...].reshape(1, D)).reshape(D)


def finish_fields(quads, grad_out, out):
    for s in range(4):
        rows = slice(0, 3) if s >= 2 else slice(3, 6)
        cols = slice(0, 6) if s % 2 else slice(6, 12)
        out[rows, cols] = (grad_out[rows, cols].astype(F32) + quads[s].astype(F32)).astype(BF)


def finish_table(rows, out):
    for k in range(26):
        width = min(128, 3312 - 128 * k)
        block = rows[k // 2].astype(F32)[8 * (k % 2) : 8 * (k % 2) + 8]
        for h in range(HEADS):
            out[h, :, 128 * k : 128 * k + width] = block[h : h + 1, 0:width]


def exchange(src_of, recv, group, send_sem, recv_sem):
    size, rank, device_of = group
    copies = []
    for k in range(1, size):
        peer = lax.rem(rank + k, size)
        copy = pltpu.make_async_remote_copy(
            src_ref=src_of(peer),
            dst_ref=recv.at[rank],
            send_sem=send_sem,
            recv_sem=recv_sem.at[k] if len(recv_sem.shape) else recv_sem,
            device_id=device_of(peer),
            device_id_type=MESH,
        )
        copy.start()
        copies.append(copy)
    return copies


def wait_bytes(ref, sem):
    pltpu.make_async_copy(ref, ref, sem).wait()


def arrive(copies):
    for copy in copies:
        copy.wait_recv()


def total_of(recv):
    total = recv[0].astype(F32)
    for k in range(1, recv.shape[0]):
        total = total + recv[k].astype(F32)
    return total


def kernel(
    fields, grad_out, ids_hbm, gain_hbm, wqkv_hbm, wproj_hbm, table_hbm,
    gather_hbm, shear_hbm, row_hbm, lon_hbm,
    out_flat, out_quads, out_table,
    ids, gain, wqkv, wproj, table, gather, shear, row_of, lon_of,
    field_in, grad_in, xs, bias, gs, stacked, ms, tflat, quads_out, quads_in,
    flat, w_out, w_in, w_half, w1, w2_out, w2, w3, t_out, t1, t2_out, t2, t3,
    block_sem, across_sem, out_sem, load_sem, own_sem, halo_send, halo_recv, back_send, back_recv,
    pair_send, pair_recv, w1_send, w1_recv, w2_send, w2_recv, w3_send, w3_recv, w4_send, w4_recv,
    t1_send, t1_recv, t2_send, t2_recv, t3_send, t3_recv,
):
    l, a = lax.axis_index("lon"), lax.axis_index("lat")
    part, block = lax.rem(l, FOUR), l // FOUR
    core, side = lax.rem(part, 2), part // 2
    near_l, far_l = lax.rem(l + 63, 64), lax.rem(l + 1, 64)
    near_a, far_a = lax.rem(a + 7, 8), lax.rem(a + 1, 8)

    inside = (INSIDE, a * 2 + side, lambda r: (block * FOUR + lax.rem(r, 2) * 2 + core, r // 2))
    across = (ACROSS, block, lambda r: (r * FOUR + part, a))
    in_four = (FOUR, part, lambda r: (block * FOUR + r, a))
    barrier = pltpu.get_barrier_semaphore()
    near = ((near_l, a), (l, near_a), (near_l, near_a))
    far = ((far_l, a), (l, far_a), (far_l, far_a))
    beside = [(near_l, a), (far_l, a), near[2], far[2]]
    column = [(l, lax.rem(a + k, 8)) for k in range(1, 8)]
    four = [(block * FOUR + lax.rem(part + k, FOUR), a) for k in range(1, FOUR)]
    high, low = block // 4, lax.rem(block, 4)
    lows = [((high * 4 + lax.rem(low + k, 4)) * FOUR + part, a) for k in range(1, 4)]
    highs = [((lax.rem(high + k, 4) * 4 + low) * FOUR + part, a) for k in range(1, 4)]
    entry = highs + lows + column + beside + four
    for device in entry:
        pl.semaphore_signal(barrier, inc=1, device_id=device, device_id_type=MESH)
    loads = []
    pairs = (
        (table_hbm, table), (shear_hbm, shear), (ids_hbm, ids), (row_hbm, row_of), (lon_hbm, lon_of),
        (gather_hbm, gather), (gain_hbm, gain), (wqkv_hbm, wqkv), (wproj_hbm, wproj),
    )
    for k, (src, dst) in enumerate(pairs):
        load = pltpu.make_async_copy(src, dst, load_sem.at[k])
        load.start()
        loads.append(load)
    owns = []
    for k, (src, dst) in enumerate(((fields, field_in), (grad_out, grad_in))):
        own = pltpu.make_async_copy(src.at[3:6, 6:12], dst.at[0], own_sem.at[k])
        own.start()
        owns.append(own)
    pl.semaphore_wait(barrier, len(entry))

    halo = []
    for s in range(1, 4):
        rows = slice(0, 3) if s >= 2 else slice(3, 6)
        cols = slice(0, 6) if s % 2 else slice(6, 12)
        for k, (src, dst) in enumerate(((fields, field_in), (grad_out, grad_in))):
            copy = pltpu.make_async_remote_copy(
                src_ref=src.at[rows, cols],
                dst_ref=dst.at[s],
                send_sem=halo_send.at[2 * s + k],
                recv_sem=halo_recv.at[2 * s + k],
                device_id=near[s - 1],
                device_id_type=MESH,
            )
            copy.start()
            halo.append(copy)

    for device in four:
        pl.semaphore_signal(block_sem, inc=1, device_id=device, device_id_type=MESH)
    for device in highs:
        pl.semaphore_signal(across_sem, inc=1, device_id=device, device_id_type=MESH)

    for load in loads:
        load.wait()
    expand_bias(table, shear, xs, bias)
    ids_p, ids_q = window_ids(ids, row_of, lon_of, ms)
    same = ids_p == ids_q
    for h in range(HEADS):
        bias[h] = jnp.where(same, bias[h], -1000000000.0)

    for own in owns:
        own.wait()
    arrive(halo)
    moved = dot(gather[...], field_in[...].reshape(TOK, D)).astype(BF)
    moved_grad = dot(gather[...], grad_in[...].reshape(TOK, D)).astype(BF)
    grad_qkv, grad_proj, local = window_grads(
        moved, moved_grad, gain[...].reshape(1, D), wqkv[...], wproj[...], bias, gs
    )

    pack_weights(grad_qkv, grad_proj, flat, w_out)
    rank = inside[1]
    pl.semaphore_wait(block_sem, FOUR - 1)
    pl.semaphore_wait(across_sem, 3)
    partner = (l + 1 - 2 * core, a)
    pair = []
    for k in range(1, INSIDE + 1):
        slot = lax.rem(rank + k, INSIDE)
        copy = pltpu.make_async_remote_copy(
            src_ref=w_out.at[1 - core, slot],
            dst_ref=w_in.at[slot],
            send_sem=pair_send,
            recv_sem=pair_recv.at[k - 1],
            device_id=partner,
            device_id_type=MESH,
        )
        copy.start()
        pair.append(copy)

    for k in range(1, INSIDE + 1):
        slot = lax.rem(rank + k, INSIDE)
        pair[k - 1].wait_recv()
        both = (w_out[core, slot].astype(F32) + w_in[slot].astype(F32)).astype(BF)
        if k == INSIDE:
            w1[slot] = both
        else:
            w_half[slot] = both
            pltpu.make_async_remote_copy(
                src_ref=w_half.at[slot],
                dst_ref=w1.at[rank],
                send_sem=w1_send,
                recv_sem=w1_recv,
                device_id=inside[2](slot),
                device_id_type=MESH,
            ).start()

    tflat[...] = jnp.zeros_like(tflat)
    fold_bias(gs, shear, stacked, xs, tflat)
    for r in range(ACROSS):
        if r < 13:
            two = [tflat[:, 256 * r : 256 * r + 128], tflat[:, 256 * r + 128 : 256 * r + 256]]
            t_out[r] = jnp.concatenate(two, axis=0).astype(BF)
        else:
            t_out[r] = jnp.zeros((16, 128), BF)
    exchange(lambda r: t_out.at[r], t1, across, t1_send, t1_recv)
    t1[block] = t_out[block]
    quads = dot_cols(gather[...], local()).astype(BF)
    quads_out[...] = quads.reshape(4, 3, 6, 2, D)
    back = []
    for s in range(1, 4):
        copy = pltpu.make_async_remote_copy(
            src_ref=quads_out.at[s],
            dst_ref=quads_in.at[s],
            send_sem=back_send.at[s],
            recv_sem=back_recv.at[s],
            device_id=far[s - 1],
            device_id_type=MESH,
        )
        copy.start()
        back.append(copy)
    quads_in[0] = quads_out[0]

    for copy in halo:
        copy.wait_send()
    wait_bytes(w_in, pair_send)

    wait_bytes(w1.at[1:], w1_recv)
    mine = total_of(w1).astype(BF)
    w2_out[...] = mine
    w2[block] = mine
    exchange(lambda r: w2_out, w2, across, w2_send, w2_recv)

    wait_bytes(t1.at[1:], t1_recv)
    mine = total_of(t1).astype(BF)
    t2_out[...] = mine
    t2[part] = mine
    exchange(lambda r: t2_out, t2, in_four, t2_send, t2_recv)
    wait_bytes(w1.at[1:], w1_send)
    wait_bytes(t1.at[1:], t1_send)
    arrive(back)
    quads_done = pltpu.make_async_copy(quads_in, out_quads, out_sem.at[1])
    quads_done.start()

    wait_bytes(t2.at[1:], t2_recv)
    t3[block] = total_of(t2).astype(BF)
    exchange(lambda r: t3.at[block], t3, across, t3_send, t3_recv)

    wait_bytes(w2.at[1:], w2_recv)
    w3[core, rank] = total_of(w2).astype(BF)
    c3 = exchange(lambda r: w3.at[core, rank], w3.at[core], inside, w3_send, w3_recv)
    for copy in back:
        copy.wait_send()
    wait_bytes(w2.at[1:], w2_send)
    wait_bytes(t2.at[1:], t2_send)

    for k in range(INSIDE):
        if k:
            c3[k - 1].wait_recv()
        slot = lax.rem(rank + INSIDE - k, INSIDE)
        pltpu.make_async_remote_copy(
            src_ref=w3.at[core, slot],
            dst_ref=out_flat.at[core, slot],
            send_sem=w4_send,
            recv_sem=w4_recv,
            device_id=partner,
            device_id_type=MESH,
        ).start()
    rows_out = pltpu.make_async_copy(w3.at[core], out_flat.at[core], out_sem.at[2])
    rows_out.start()
    wait_bytes(t3.at[1:], t3_recv)
    table_out = pltpu.make_async_copy(t3, out_table, out_sem.at[0])
    table_out.start()
    wait_bytes(t3.at[1:], t3_send)
    wait_bytes(w1.at[1:], w3_send)
    wait_bytes(w1, w4_recv)
    wait_bytes(w1, w4_send)
    quads_done.wait()
    table_out.wait()
    rows_out.wait()


def finish(rows, quads, trows, grad_out, wqkv, gain, out_f, out_qkv, out_proj, out_gain, out_t, flat):
    finish_weights(rows, wqkv, gain, flat, out_qkv, out_proj, out_gain)
    finish_fields(quads, grad_out, out_f)
    finish_table(trows, out_t)


def body(fields, grad_out, mask_ids, ln_gain, qkv_weight, proj_weight, bias_table):
    consts = [jnp.asarray(v, BF) for v in token_tables()]
    fields = jnp.transpose(fields, (1, 2, 0, 3))
    grad_out = jnp.transpose(grad_out, (1, 2, 0, 3))
    vmem = pl.BlockSpec(memory_space=pltpu.VMEM)
    hbm = pl.BlockSpec(memory_space=pl.ANY)
    dma = pltpu.SemaphoreType.DMA
    scratch = [
        pltpu.VMEM((6, 2, 12), jnp.int32),
        pltpu.VMEM((D,), F32),
        pltpu.VMEM((D, 576), BF),
        pltpu.VMEM((D, D), BF),
        pltpu.VMEM((HEADS, 1, 3312), F32),
        pltpu.VMEM((TOK, TOK), BF),
        pltpu.VMEM((512, 384), BF),
        pltpu.VMEM((TOK, 16), BF),
        pltpu.VMEM((TOK, 128), BF),
        pltpu.VMEM((4, 3, 6, 2, D), BF),
        pltpu.VMEM((4, 3, 6, 2, D), BF),
        pltpu.VMEM((4, 72, 128), F32),
        pltpu.VMEM((HEADS, TOK, TOK), F32),
        pltpu.VMEM((HEADS, TOK, TOK), F32),
        pltpu.VMEM((LON, 72, TOK), F32),
        pltpu.VMEM((16, 128), F32),
        pltpu.VMEM((8, 3328), F32),
        pltpu.VMEM((4, 3, 6, 2, D), BF),
        pltpu.VMEM((4, 3, 6, 2, D), BF),
        pltpu.VMEM((1152, 128), F32),
        pltpu.VMEM((2, INSIDE, ROWS, 128), BF),
        pltpu.VMEM((INSIDE, ROWS, 128), BF),
        pltpu.VMEM((INSIDE, ROWS, 128), BF),
        pltpu.VMEM((INSIDE, ROWS, 128), BF),
        pltpu.VMEM((ROWS, 128), BF),
        pltpu.VMEM((ACROSS, ROWS, 128), BF),
        pltpu.VMEM((2, INSIDE, ROWS, 128), BF),
        pltpu.VMEM((ACROSS, 16, 128), BF),
        pltpu.VMEM((ACROSS, 16, 128), BF),
        pltpu.VMEM((16, 128), BF),
        pltpu.VMEM((FOUR, 16, 128), BF),
        pltpu.VMEM((ACROSS, 16, 128), BF),
        pltpu.SemaphoreType.REGULAR,
        pltpu.SemaphoreType.REGULAR,
        dma((3,)),
        dma((9,)),
        dma((2,)),
        dma((8,)),
        dma((8,)),
        dma((4,)),
        dma((4,)),
        dma,
        dma((INSIDE,)),
        *([dma] * 5),
        dma((INSIDE,)),
        *([dma] * 8),
    ]
    rows, quads, trows = pl.pallas_call(
        kernel,
        out_shape=(
            jax.ShapeDtypeStruct((2, INSIDE, ROWS, 128), BF),
            jax.ShapeDtypeStruct((4, 3, 6, 2, D), BF),
            jax.ShapeDtypeStruct((ACROSS, 16, 128), BF),
        ),
        in_specs=[hbm] * 11,
        out_specs=(hbm, hbm, hbm),
        scratch_shapes=scratch,
        compiler_params=pltpu.CompilerParams(
            collective_id=0, has_side_effects=True, vmem_limit_bytes=VMEM_LIMIT
        ),
    )(
        fields, grad_out, jnp.transpose(mask_ids, (1, 0, 2)), ln_gain, qkv_weight, proj_weight,
        bias_table.reshape(HEADS, 1, 3312), *consts,
    )
    out_f, out_qkv, out_proj, out_gain, out_t = pl.pallas_call(
        finish,
        out_shape=(
            jax.ShapeDtypeStruct((6, 12, 2, D), BF),
            jax.ShapeDtypeStruct((D, 576), F32),
            jax.ShapeDtypeStruct((D, D), F32),
            jax.ShapeDtypeStruct((D,), F32),
            jax.ShapeDtypeStruct((HEADS, 1, 3312), F32),
        ),
        in_specs=[vmem] * 6,
        out_specs=(vmem,) * 5,
        scratch_shapes=[pltpu.VMEM((1152, 128), F32)],
        compiler_params=pltpu.CompilerParams(vmem_limit_bytes=VMEM_LIMIT),
    )(rows, quads, trows, grad_out, qkv_weight, ln_gain)
    out_f = jnp.transpose(out_f, (2, 0, 1, 3))
    return out_f, out_qkv, out_proj, out_gain, out_t.reshape(1, 1, HEADS, 3312)


def solution(mesh):
    placed = (
        P(None, "lat", "lon", None),
        P(None, "lat", "lon", None),
        P(None, "lat", "lon"),
        P(),
        P(),
        P(),
        P("lat", None, None, None),
    )
    return jax.shard_map(
        body,
        mesh=mesh,
        in_specs=placed,
        out_specs=(P(None, "lat", "lon", None), P(), P(), P(), P("lat", None, None, None)),
        check_vma=False,
    )
```

```python
import functools

import jax
import jax.numpy as jnp
import numpy as np
from jax import lax
from jax.experimental import pallas as pl
from jax.experimental.pallas import tpu as pltpu
from jax.sharding import PartitionSpec as P

D = 192
HEADS = 6
LON = 12
CELLS = 12
TOK = 144
SPAN = 23 * CELLS
SEG = 138
EPS = 1e-05
MESH = pl.DeviceIdType.MESH
BF = jnp.bfloat16
F32 = jnp.float32

INSIDE, ACROSS, FOUR = 16, 16, 4
ROWS = 1152 // (2 * INSIDE)
VMEM_LIMIT = 60 * 1024 * 1024


def token_tables():
    gather = np.zeros((TOK, TOK), np.float32)
    for o in range(12):
        for z in range(2):
            for a in range(6):
                s = (a >= 3) * 2 + (o >= 6)
                gather[o * 12 + z * 6 + a, ((s * 3 + a % 3) * 6 + o % 6) * 2 + (z + 1) % 2] = 1
    shear = np.zeros((512, 384), np.float32)
    for zq in range(2):
        for aq in range(6):
            for r in range(23):
                shear[zq * 256 + aq * 23 + r, r * 12 + zq * 6 + aq] = 1
    row_of = np.zeros((TOK, 16), np.float32)
    lon_of = np.zeros((TOK, 128), np.float32)
    for t in range(TOK):
        row_of[t, t % 12] = 1
        lon_of[t, t // 12] = 1
    return gather, shear, row_of, lon_of


def dot(a, b):
    return lax.dot_general(a, b, (((1,), (0,)), ((), ())), preferred_element_type=F32)


def dot_rows(a, b):
    return lax.dot_general(a, b, (((1,), (1,)), ((), ())), preferred_element_type=F32)


def dot_cols(a, b):
    return lax.dot_general(a, b, (((0,), (0,)), ((), ())), preferred_element_type=F32)


def split(v):
    hi = v.astype(BF)
    return hi, (v - hi.astype(F32)).astype(BF)


def expand_bias(table, shear, xs, bias):
    for zp in range(2):
        for zq in range(2):
            for ap in range(6):
                start = ((zp * 2 + zq) * 6 + ap) * SEG
                rows = pl.ds(zp * 6 + ap, HEADS, stride=CELLS)
                part = table[:, 0, start : start + SEG]
                rest = jnp.concatenate([part[:, 128:], jnp.zeros((HEADS, 256 - SEG), F32)], axis=1)
                xs[2 * zq, rows, :] = part[:, 0:128]
                xs[2 * zq + 1, rows, :] = rest
    hi, lo = split(jnp.concatenate([xs[k, 0:72] for k in range(4)], axis=1))
    sheared = dot(hi, shear[...]) + dot(lo, shear[...])
    for op in range(LON):
        window = sheared[:, (11 - op) * 12 : (11 - op) * 12 + TOK]
        for h in range(HEADS):
            bias[h, op * 12 : (op + 1) * 12, :] = window[h * 12 : (h + 1) * 12]


def fold_bias(gs, shear, stacked, xs, flat):
    for op in range(LON):
        for h in range(HEADS):
            stacked[op, h * 12 : (h + 1) * 12, :] = gs[h, op * 12 : (op + 1) * 12, :]
    total = None
    for op in range(LON):
        left = (11 - op) * 12
        parts = [stacked[op]]
        if left:
            parts.insert(0, jnp.zeros((72, left), F32))
        if SPAN - left - TOK:
            parts.append(jnp.zeros((72, SPAN - left - TOK), F32))
        piece = jnp.concatenate(parts, axis=1) if len(parts) > 1 else parts[0]
        total = piece if total is None else total + piece
    total = jnp.concatenate([total, jnp.zeros((72, 384 - SPAN), F32)], axis=1)
    hi, lo = split(total)
    spread = dot_rows(hi, shear[...]) + dot_rows(lo, shear[...])
    for k in range(4):
        xs[k, 0:72] = spread[:, 128 * k : 128 * k + 128]
    for zp in range(2):
        for zq in range(2):
            for ap in range(6):
                start = ((zp * 2 + zq) * 6 + ap) * SEG
                rows = pl.ds(zp * 6 + ap, HEADS, stride=CELLS)
                flat[0:HEADS, start : start + 128] = xs[2 * zq, rows, :]
                flat[0:HEADS, start + 128 : start + SEG] = xs[2 * zq + 1, rows, :][:, 0 : SEG - 128]


def window_ids(ids, row_of, lon_of, ms):
    ms[...] = jnp.zeros_like(ms)
    for a in range(6):
        ms[a : a + 1, 0:12] = ids[a, 0:1].astype(F32)
        ms[a + 6 : a + 7, 0:12] = ids[a, 1:2].astype(F32)
    m = ms[...].astype(BF)
    column = jnp.sum(dot(row_of[...], m) * lon_of[...].astype(F32), axis=1, keepdims=True)
    spread = dot_cols(m, row_of[...].astype(F32).T.astype(BF))
    row = jnp.sum(spread * lon_of[...].astype(F32).T, axis=0, keepdims=True)
    return column, row


def window_grads(x, g, gain, wqkv, wproj, bias, gs_out):
    x = x.astype(F32)
    centred = x - jnp.mean(x, axis=-1, keepdims=True)
    inv_std = lax.rsqrt(jnp.mean(centred * centred, axis=-1, keepdims=True) + EPS)
    normed = centred * inv_std
    hidden = (normed * gain).astype(BF)
    projected = dot(hidden, wqkv)
    scaling = 32 ** (-0.5)
    query = (projected[:, :D] * scaling).astype(BF)
    key = projected[:, D : 2 * D].astype(BF)
    value = projected[:, 2 * D :].astype(BF)
    grad_att = dot_rows(g, wproj).astype(BF)
    lane = lax.broadcasted_iota(jnp.int32, (TOK, D), 1) // 32
    zero = jnp.zeros((TOK, D), BF)
    heads = range(HEADS)

    def by_head(v):
        return [jnp.where(lane == h, v, zero) for h in heads]

    def stack(v):
        return jnp.concatenate(v, axis=0)

    def unstack(v):
        return [v[h * TOK : (h + 1) * TOK] for h in heads]

    def over_heads(left, right):
        total = dot(left[0], right[0])
        for h in range(1, HEADS):
            total = total + dot(left[h], right[h])
        return total

    queries, grads = stack(by_head(query)), stack(by_head(grad_att))
    scores = unstack(dot_rows(queries, key))
    grad_prob = unstack(dot_rows(grads, value))
    scores = [scores[h] + bias[h] for h in heads]
    raised = [jnp.exp(v - jnp.max(v, axis=-1, keepdims=True)) for v in scores]
    prob = [v * (1.0 / jnp.sum(v, axis=-1, keepdims=True)) for v in raised]
    prob_bf = [v.astype(BF) for v in prob]
    weighted = [prob[h] * grad_prob[h] for h in heads]
    gs = [w - p * jnp.sum(w, axis=-1, keepdims=True) for w, p in zip(weighted, prob)]
    for h in heads:
        gs_out[h] = gs[h]
    gs = [v.astype(BF) for v in gs]
    attended = over_heads(prob_bf, by_head(value))
    dv = dot_cols(stack(prob_bf), grads)
    dq = over_heads(gs, by_head(key))
    dk = dot_cols(stack(gs), queries)
    joint = jnp.concatenate(
        [(dq * scaling).astype(BF), dk.astype(BF), dv.astype(BF)], axis=1
    )
    grad_qkv = dot_cols(hidden, joint)
    grad_proj = dot_cols(attended.astype(BF), g)

    def local():
        grad_hidden = dot_rows(joint, wqkv)
        scaled = grad_hidden * gain
        return (
            inv_std
            * (
                scaled
                - jnp.mean(scaled, axis=-1, keepdims=True)
                - normed * jnp.mean(scaled * normed, axis=-1, keepdims=True)
            )
        ).astype(BF)

    return grad_qkv, grad_proj, local


def pack_weights(grad_qkv, grad_proj, flat, out):
    for c in range(4):
        flat[c * 192 : (c + 1) * 192, :] = grad_qkv[:, c * 128 : (c + 1) * 128]
    flat[768:960, :] = jnp.concatenate([grad_qkv[:, 512:576], grad_proj[:, 128:192]], axis=1)
    flat[960:1152, :] = grad_proj[:, 0:128]
    for r in range(2 * INSIDE):
        out[r // INSIDE, r % INSIDE] = flat[ROWS * r : ROWS * (r + 1), :].astype(BF)


def finish_weights(rows, wqkv, gain, flat, out_qkv, out_proj, out_gain):
    for r in range(2 * INSIDE):
        flat[ROWS * r : ROWS * (r + 1), :] = rows[r // INSIDE, r % INSIDE].astype(F32)
    for c in range(4):
        out_qkv[:, c * 128 : (c + 1) * 128] = flat[c * 192 : (c + 1) * 192, :]
    last = flat[768:960, :]
    out_qkv[:, 512:576] = last[:, 0:64]
    out_proj[:, 128:192] = last[:, 64:128]
    out_proj[:, 0:128] = flat[960:1152, :]
    products = out_qkv[...] * wqkv[...].astype(F32)
    hi, lo = split(products)
    ones = jnp.ones((8, 576), BF)
    row = (dot_rows(ones, hi) + dot_rows(ones, lo))[0:1]
    out_gain[...] = (row / gain[...].reshape(1, D)).reshape(D)


def finish_fields(quads, grad_out, out):
    for s in range(4):
        rows = slice(0, 3) if s >= 2 else slice(3, 6)
        cols = slice(0, 6) if s % 2 else slice(6, 12)
        out[rows, cols] = (grad_out[rows, cols].astype(F32) + quads[s].astype(F32)).astype(BF)


def finish_table(rows, out):
    for k in range(26):
        width = min(128, 3312 - 128 * k)
        block = rows[k // 2].astype(F32)[8 * (k % 2) : 8 * (k % 2) + 8]
        for h in range(HEADS):
            out[h, :, 128 * k : 128 * k + width] = block[h : h + 1, 0:width]


def exchange(src_of, recv, group, send_sem, recv_sem):
    size, rank, device_of = group
    copies = []
    for k in range(1, size):
        peer = lax.rem(rank + k, size)
        copy = pltpu.make_async_remote_copy(
            src_ref=src_of(peer),
            dst_ref=recv.at[rank],
            send_sem=send_sem,
            recv_sem=recv_sem.at[k] if len(recv_sem.shape) else recv_sem,
            device_id=device_of(peer),
            device_id_type=MESH,
        )
        copy.start()
        copies.append(copy)
    return copies


def wait_bytes(ref, sem):
    pltpu.make_async_copy(ref, ref, sem).wait()


def arrive(copies):
    for copy in copies:
        copy.wait_recv()


def total_of(recv):
    total = recv[0].astype(F32)
    for k in range(1, recv.shape[0]):
        total = total + recv[k].astype(F32)
    return total


def kernel(
    fields, grad_out, ids_hbm, gain_hbm, wqkv_hbm, wproj_hbm, table_hbm,
    gather_hbm, shear_hbm, row_hbm, lon_hbm,
    out_flat, out_quads, out_table,
    ids, gain, wqkv, wproj, table, gather, shear, row_of, lon_of,
    field_in, grad_in, xs, bias, gs, stacked, ms, tflat, quads_out, quads_in,
    flat, w_out, w_in, w_half, w1, w2_out, w2, w3, t_out, t1, t2_out, t2, t3,
    block_sem, across_sem, out_sem, load_sem, own_sem, halo_send, halo_recv, back_send, back_recv,
    pair_send, pair_recv, w1_send, w1_recv, w2_send, w2_recv, w3_send, w3_recv, w4_send, w4_recv,
    t1_send, t1_recv, t2_send, t2_recv, t3_send, t3_recv,
):
    l, a = lax.axis_index("lon"), lax.axis_index("lat")
    part, block = lax.rem(l, FOUR), l // FOUR
    core, side = lax.rem(part, 2), part // 2
    near_l, far_l = lax.rem(l + 63, 64), lax.rem(l + 1, 64)
    near_a, far_a = lax.rem(a + 7, 8), lax.rem(a + 1, 8)

    inside = (INSIDE, a * 2 + side, lambda r: (block * FOUR + lax.rem(r, 2) * 2 + core, r // 2))
    across = (ACROSS, block, lambda r: (r * FOUR + part, a))
    in_four = (FOUR, part, lambda r: (block * FOUR + r, a))
    barrier = pltpu.get_barrier_semaphore()
    near = ((near_l, a), (l, near_a), (near_l, near_a))
    far = ((far_l, a), (l, far_a), (far_l, far_a))
    beside = [(near_l, a), (far_l, a), near[2], far[2]]
    column = [(l, lax.rem(a + k, 8)) for k in range(1, 8)]
    four = [(block * FOUR + lax.rem(part + k, FOUR), a) for k in range(1, FOUR)]
    high, low = block // 4, lax.rem(block, 4)
    lows = [((high * 4 + lax.rem(low + k, 4)) * FOUR + part, a) for k in range(1, 4)]
    highs = [((lax.rem(high + k, 4) * 4 + low) * FOUR + part, a) for k in range(1, 4)]
    entry = highs + lows + column + beside + four
    for device in entry:
        pl.semaphore_signal(barrier, inc=1, device_id=device, device_id_type=MESH)
    loads = []
    pairs = (
        (table_hbm, table), (shear_hbm, shear), (ids_hbm, ids), (row_hbm, row_of), (lon_hbm, lon_of),
        (gather_hbm, gather), (gain_hbm, gain), (wqkv_hbm, wqkv), (wproj_hbm, wproj),
    )
    for k, (src, dst) in enumerate(pairs):
        load = pltpu.make_async_copy(src, dst, load_sem.at[k])
        load.start()
        loads.append(load)
    owns = []
    for k, (src, dst) in enumerate(((fields, field_in), (grad_out, grad_in))):
        own = pltpu.make_async_copy(src.at[3:6, 6:12], dst.at[0], own_sem.at[k])
        own.start()
        owns.append(own)
    pl.semaphore_wait(barrier, len(entry))

    for s in range(1, 4):
        rows = slice(0, 3) if s >= 2 else slice(3, 6)
        cols = slice(0, 6) if s % 2 else slice(6, 12)
        for k, (src, dst) in enumerate(((fields, field_in), (grad_out, grad_in))):
            copy = pltpu.make_async_remote_copy(
                src_ref=src.at[rows, cols],
                dst_ref=dst.at[s],
                send_sem=halo_send.at[k],
                recv_sem=halo_recv.at[k],
                device_id=near[s - 1],
                device_id_type=MESH,
            )
            copy.start()

    for device in four:
        pl.semaphore_signal(block_sem, inc=1, device_id=device, device_id_type=MESH)
    for device in highs:
        pl.semaphore_signal(across_sem, inc=1, device_id=device, device_id_type=MESH)

    for load in loads:
        load.wait()
    expand_bias(table, shear, xs, bias)
    ids_p, ids_q = window_ids(ids, row_of, lon_of, ms)
    same = ids_p == ids_q
    for h in range(HEADS):
        bias[h] = jnp.where(same, bias[h], -1000000000.0)

    for own in owns:
        own.wait()
    wait_bytes(field_in.at[1:], halo_recv.at[0])
    wait_bytes(grad_in.at[1:], halo_recv.at[1])
    moved = dot(gather[...], field_in[...].reshape(TOK, D)).astype(BF)
    moved_grad = dot(gather[...], grad_in[...].reshape(TOK, D)).astype(BF)
    grad_qkv, grad_proj, local = window_grads(
        moved, moved_grad, gain[...].reshape(1, D), wqkv[...], wproj[...], bias, gs
    )

    pack_weights(grad_qkv, grad_proj, flat, w_out)
    rank = inside[1]
    pl.semaphore_wait(block_sem, FOUR - 1)
    pl.semaphore_wait(across_sem, 3)
    partner = (l + 1 - 2 * core, a)
    pair = []
    for k in range(1, 5):
        group = lax.rem(rank // 4 + k, 4)
        four_rows = pl.ds(pl.multiple_of(group * 4, 4), 4)
        copy = pltpu.make_async_remote_copy(
            src_ref=w_out.at[1 - core, four_rows],
            dst_ref=w_in.at[four_rows],
            send_sem=pair_send,
            recv_sem=pair_recv.at[k - 1],
            device_id=partner,
            device_id_type=MESH,
        )
        copy.start()
        pair.append(copy)

    for k in range(1, 5):
        group = lax.rem(rank // 4 + k, 4)
        pair[k - 1].wait_recv()
        for j in range(1, 5):
            slot = group * 4 + lax.rem(rank + j, 4)
            both = (w_out[core, slot].astype(F32) + w_in[slot].astype(F32)).astype(BF)
            if k == 4 and j == 4:
                w1[rank] = both
            else:
                w_half[slot] = both
                pltpu.make_async_remote_copy(
                    src_ref=w_half.at[slot],
                    dst_ref=w1.at[rank],
                    send_sem=w1_send,
                    recv_sem=w1_recv,
                    device_id=inside[2](slot),
                    device_id_type=MESH,
                ).start()

    tflat[...] = jnp.zeros_like(tflat)
    fold_bias(gs, shear, stacked, xs, tflat)
    for r in range(ACROSS):
        if r < 13:
            two = [tflat[:, 256 * r : 256 * r + 128], tflat[:, 256 * r + 128 : 256 * r + 256]]
            t_out[r] = jnp.concatenate(two, axis=0).astype(BF)
        else:
            t_out[r] = jnp.zeros((16, 128), BF)
    exchange(lambda r: t_out.at[r], t1, across, t1_send, t1_recv)
    t1[block] = t_out[block]
    quads = dot_cols(gather[...], local()).astype(BF)
    quads_out[...] = quads.reshape(4, 3, 6, 2, D)
    back = []
    for s in range(1, 4):
        copy = pltpu.make_async_remote_copy(
            src_ref=quads_out.at[s],
            dst_ref=quads_in.at[s],
            send_sem=back_send.at[s],
            recv_sem=back_recv.at[s],
            device_id=far[s - 1],
            device_id_type=MESH,
        )
        copy.start()
        back.append(copy)
    quads_in[0] = quads_out[0]

    wait_bytes(field_in.at[1:], halo_send.at[0])
    wait_bytes(grad_in.at[1:], halo_send.at[1])
    wait_bytes(w_in, pair_send)

    wait_bytes(w1.at[1:], w1_recv)
    mine = total_of(w1).astype(BF)
    w2_out[...] = mine
    w2[block] = mine
    exchange(lambda r: w2_out, w2, across, w2_send, w2_recv)

    wait_bytes(t1.at[1:], t1_recv)
    mine = total_of(t1).astype(BF)
    t2_out[...] = mine
    t2[part] = mine
    exchange(lambda r: t2_out, t2, in_four, t2_send, t2_recv)
    wait_bytes(w1.at[1:], w1_send)
    wait_bytes(t1.at[1:], t1_send)
    arrive(back)
    quads_done = pltpu.make_async_copy(quads_in, out_quads, out_sem.at[1])
    quads_done.start()

    wait_bytes(t2.at[1:], t2_recv)
    t3[block] = total_of(t2).astype(BF)
    exchange(lambda r: t3.at[block], t3, across, t3_send, t3_recv)

    wait_bytes(w2.at[1:], w2_recv)
    w3[core, rank] = total_of(w2).astype(BF)
    c3 = exchange(lambda r: w3.at[core, rank], w3.at[core], inside, w3_send, w3_recv)
    for copy in back:
        copy.wait_send()
    wait_bytes(w2.at[1:], w2_send)
    wait_bytes(t2.at[1:], t2_send)

    for k in range(INSIDE):
        if k:
            c3[k - 1].wait_recv()
        slot = lax.rem(rank + INSIDE - k, INSIDE)
        pltpu.make_async_remote_copy(
            src_ref=w3.at[core, slot],
            dst_ref=out_flat.at[core, slot],
            send_sem=w4_send,
            recv_sem=w4_recv,
            device_id=partner,
            device_id_type=MESH,
        ).start()
    rows_out = pltpu.make_async_copy(w3.at[core], out_flat.at[core], out_sem.at[2])
    rows_out.start()
    wait_bytes(t3.at[1:], t3_recv)
    table_out = pltpu.make_async_copy(t3, out_table, out_sem.at[0])
    table_out.start()
    wait_bytes(t3.at[1:], t3_send)
    wait_bytes(w1.at[1:], w3_send)
    wait_bytes(w1, w4_recv)
    wait_bytes(w1, w4_send)
    quads_done.wait()
    table_out.wait()
    rows_out.wait()


def finish(rows, quads, trows, grad_out, wqkv, gain, out_f, out_qkv, out_proj, out_gain, out_t, flat):
    finish_weights(rows, wqkv, gain, flat, out_qkv, out_proj, out_gain)
    finish_fields(quads, grad_out, out_f)
    finish_table(trows, out_t)


def body(fields, grad_out, mask_ids, ln_gain, qkv_weight, proj_weight, bias_table):
    consts = [jnp.asarray(v, BF) for v in token_tables()]
    fields = jnp.transpose(fields, (1, 2, 0, 3))
    grad_out = jnp.transpose(grad_out, (1, 2, 0, 3))
    vmem = pl.BlockSpec(memory_space=pltpu.VMEM)
    hbm = pl.BlockSpec(memory_space=pl.ANY)
    dma = pltpu.SemaphoreType.DMA
    scratch = [
        pltpu.VMEM((6, 2, 12), jnp.int32),
        pltpu.VMEM((D,), F32),
        pltpu.VMEM((D, 576), BF),
        pltpu.VMEM((D, D), BF),
        pltpu.VMEM((HEADS, 1, 3312), F32),
        pltpu.VMEM((TOK, TOK), BF),
        pltpu.VMEM((512, 384), BF),
        pltpu.VMEM((TOK, 16), BF),
        pltpu.VMEM((TOK, 128), BF),
        pltpu.VMEM((4, 3, 6, 2, D), BF),
        pltpu.VMEM((4, 3, 6, 2, D), BF),
        pltpu.VMEM((4, 96, 128), F32),
        pltpu.VMEM((HEADS, TOK, TOK), F32),
        pltpu.VMEM((HEADS, TOK, TOK), F32),
        pltpu.VMEM((LON, 72, TOK), F32),
        pltpu.VMEM((16, 128), F32),
        pltpu.VMEM((8, 3328), F32),
        pltpu.VMEM((4, 3, 6, 2, D), BF),
        pltpu.VMEM((4, 3, 6, 2, D), BF),
        pltpu.VMEM((1152, 128), F32),
        pltpu.VMEM((2, INSIDE, ROWS, 128), BF),
        pltpu.VMEM((INSIDE, ROWS, 128), BF),
        pltpu.VMEM((INSIDE, ROWS, 128), BF),
        pltpu.VMEM((INSIDE, ROWS, 128), BF),
        pltpu.VMEM((ROWS, 128), BF),
        pltpu.VMEM((ACROSS, ROWS, 128), BF),
        pltpu.VMEM((2, INSIDE, ROWS, 128), BF),
        pltpu.VMEM((ACROSS, 16, 128), BF),
        pltpu.VMEM((ACROSS, 16, 128), BF),
        pltpu.VMEM((16, 128), BF),
        pltpu.VMEM((FOUR, 16, 128), BF),
        pltpu.VMEM((ACROSS, 16, 128), BF),
        pltpu.SemaphoreType.REGULAR,
        pltpu.SemaphoreType.REGULAR,
        dma((3,)),
        dma((9,)),
        dma((2,)),
        dma((2,)),
        dma((2,)),
        dma((4,)),
        dma((4,)),
        dma,
        dma((4,)),
        *([dma] * 5),
        dma((INSIDE,)),
        *([dma] * 8),
    ]
    rows, quads, trows = pl.pallas_call(
        kernel,
        out_shape=(
            jax.ShapeDtypeStruct((2, INSIDE, ROWS, 128), BF),
            jax.ShapeDtypeStruct((4, 3, 6, 2, D), BF),
            jax.ShapeDtypeStruct((ACROSS, 16, 128), BF),
        ),
        in_specs=[hbm] * 11,
        out_specs=(hbm, hbm, hbm),
        scratch_shapes=scratch,
        compiler_params=pltpu.CompilerParams(
            collective_id=0, has_side_effects=True, vmem_limit_bytes=VMEM_LIMIT
        ),
    )(
        fields, grad_out, jnp.transpose(mask_ids, (1, 0, 2)), ln_gain, qkv_weight, proj_weight,
        bias_table.reshape(HEADS, 1, 3312), *consts,
    )
    out_f, out_qkv, out_proj, out_gain, out_t = pl.pallas_call(
        finish,
        out_shape=(
            jax.ShapeDtypeStruct((6, 12, 2, D), BF),
            jax.ShapeDtypeStruct((D, 576), F32),
            jax.ShapeDtypeStruct((D, D), F32),
            jax.ShapeDtypeStruct((D,), F32),
            jax.ShapeDtypeStruct((HEADS, 1, 3312), F32),
        ),
        in_specs=[vmem] * 6,
        out_specs=(vmem,) * 5,
        scratch_shapes=[pltpu.VMEM((1152, 128), F32)],
        compiler_params=pltpu.CompilerParams(vmem_limit_bytes=VMEM_LIMIT),
    )(rows, quads, trows, grad_out, qkv_weight, ln_gain)
    out_f = jnp.transpose(out_f, (2, 0, 1, 3))
    return out_f, out_qkv, out_proj, out_gain, out_t.reshape(1, 1, HEADS, 3312)


def solution(mesh):
    placed = (
        P(None, "lat", "lon", None),
        P(None, "lat", "lon", None),
        P(None, "lat", "lon"),
        P(),
        P(),
        P(),
        P("lat", None, None, None),
    )
    return jax.shard_map(
        body,
        mesh=mesh,
        in_specs=placed,
        out_specs=(P(None, "lat", "lon", None), P(), P(), P(), P("lat", None, None, None)),
        check_vma=False,
    )
```

```python
import functools

import jax
import jax.numpy as jnp
import numpy as np
from jax import lax
from jax.experimental import pallas as pl
from jax.experimental.pallas import tpu as pltpu
from jax.sharding import PartitionSpec as P

D = 192
HEADS = 6
LON = 12
CELLS = 12
TOK = 144
SPAN = 23 * CELLS
SEG = 138
EPS = 1e-05
MESH = pl.DeviceIdType.MESH
BF = jnp.bfloat16
F32 = jnp.float32

INSIDE, ACROSS, FOUR = 16, 16, 4
ROWS = 1152 // (2 * INSIDE)
VMEM_LIMIT = 60 * 1024 * 1024


def token_tables():
    gather = np.zeros((TOK, TOK), np.float32)
    for o in range(12):
        for z in range(2):
            for a in range(6):
                s = (a >= 3) * 2 + (o >= 6)
                gather[o * 12 + z * 6 + a, ((s * 3 + a % 3) * 6 + o % 6) * 2 + (z + 1) % 2] = 1
    shear = np.zeros((512, 384), np.float32)
    for zq in range(2):
        for aq in range(6):
            for r in range(23):
                shear[zq * 256 + aq * 23 + r, r * 12 + zq * 6 + aq] = 1
    row_of = np.zeros((TOK, 16), np.float32)
    lon_of = np.zeros((TOK, 128), np.float32)
    for t in range(TOK):
        row_of[t, t % 12] = 1
        lon_of[t, t // 12] = 1
    return gather, shear, row_of, lon_of


def dot(a, b):
    return lax.dot_general(a, b, (((1,), (0,)), ((), ())), preferred_element_type=F32)


def dot_rows(a, b):
    return lax.dot_general(a, b, (((1,), (1,)), ((), ())), preferred_element_type=F32)


def dot_cols(a, b):
    return lax.dot_general(a, b, (((0,), (0,)), ((), ())), preferred_element_type=F32)


def split(v):
    hi = v.astype(BF)
    return hi, (v - hi.astype(F32)).astype(BF)


def expand_bias(table, shear, xs, bias):
    for zp in range(2):
        for zq in range(2):
            for ap in range(6):
                start = ((zp * 2 + zq) * 6 + ap) * SEG
                rows = pl.ds(zp * 6 + ap, HEADS, stride=CELLS)
                part = table[:, 0, start : start + SEG]
                rest = jnp.concatenate([part[:, 128:], jnp.zeros((HEADS, 256 - SEG), F32)], axis=1)
                xs[2 * zq, rows, :] = part[:, 0:128]
                xs[2 * zq + 1, rows, :] = rest
    hi, lo = split(jnp.concatenate([xs[k, 0:72] for k in range(4)], axis=1))
    sheared = dot(hi, shear[...]) + dot(lo, shear[...])
    for op in range(LON):
        window = sheared[:, (11 - op) * 12 : (11 - op) * 12 + TOK]
        for h in range(HEADS):
            bias[h, op * 12 : (op + 1) * 12, :] = window[h * 12 : (h + 1) * 12]


def fold_bias(gs, shear, stacked, xs, flat):
    for op in range(LON):
        for h in range(HEADS):
            stacked[op, h * 12 : (h + 1) * 12, :] = gs[h, op * 12 : (op + 1) * 12, :]
    total = None
    for op in range(LON):
        left = (11 - op) * 12
        parts = [stacked[op]]
        if left:
            parts.insert(0, jnp.zeros((72, left), F32))
        if SPAN - left - TOK:
            parts.append(jnp.zeros((72, SPAN - left - TOK), F32))
        piece = jnp.concatenate(parts, axis=1) if len(parts) > 1 else parts[0]
        total = piece if total is None else total + piece
    total = jnp.concatenate([total, jnp.zeros((72, 384 - SPAN), F32)], axis=1)
    hi, lo = split(total)
    spread = dot_rows(hi, shear[...]) + dot_rows(lo, shear[...])
    for k in range(4):
        xs[k, 0:72] = spread[:, 128 * k : 128 * k + 128]
    for zp in range(2):
        for zq in range(2):
            for ap in range(6):
                start = ((zp * 2 + zq) * 6 + ap) * SEG
                rows = pl.ds(zp * 6 + ap, HEADS, stride=CELLS)
                flat[0:HEADS, start : start + 128] = xs[2 * zq, rows, :]
                flat[0:HEADS, start + 128 : start + SEG] = xs[2 * zq + 1, rows, :][:, 0 : SEG - 128]


def window_ids(ids, row_of, lon_of, ms):
    ms[...] = jnp.zeros_like(ms)
    for a in range(6):
        ms[a : a + 1, 0:12] = ids[a, 0:1].astype(F32)
        ms[a + 6 : a + 7, 0:12] = ids[a, 1:2].astype(F32)
    m = ms[...].astype(BF)
    column = jnp.sum(dot(row_of[...], m) * lon_of[...].astype(F32), axis=1, keepdims=True)
    spread = dot_cols(m, row_of[...].astype(F32).T.astype(BF))
    row = jnp.sum(spread * lon_of[...].astype(F32).T, axis=0, keepdims=True)
    return column, row


def window_grads(x, g, gain, wqkv, wproj, bias, gs_out):
    x = x.astype(F32)
    centred = x - jnp.mean(x, axis=-1, keepdims=True)
    inv_std = lax.rsqrt(jnp.mean(centred * centred, axis=-1, keepdims=True) + EPS)
    normed = centred * inv_std
    hidden = (normed * gain).astype(BF)
    projected = dot(hidden, wqkv)
    scaling = 32 ** (-0.5)
    query = (projected[:, :D] * scaling).astype(BF)
    key = projected[:, D : 2 * D].astype(BF)
    value = projected[:, 2 * D :].astype(BF)
    grad_att = dot_rows(g, wproj).astype(BF)
    lane = lax.broadcasted_iota(jnp.int32, (TOK, D), 1) // 32
    zero = jnp.zeros((TOK, D), BF)
    heads = range(HEADS)

    def by_head(v):
        return [jnp.where(lane == h, v, zero) for h in heads]

    def stack(v):
        return jnp.concatenate(v, axis=0)

    def unstack(v):
        return [v[h * TOK : (h + 1) * TOK] for h in heads]

    def over_heads(left, right):
        total = dot(left[0], right[0])
        for h in range(1, HEADS):
            total = total + dot(left[h], right[h])
        return total

    queries, grads = stack(by_head(query)), stack(by_head(grad_att))
    scores = unstack(dot_rows(queries, key))
    grad_prob = unstack(dot_rows(grads, value))
    scores = [scores[h] + bias[h] for h in heads]
    raised = [jnp.exp(v - jnp.max(v, axis=-1, keepdims=True)) for v in scores]
    prob = [v * (1.0 / jnp.sum(v, axis=-1, keepdims=True)) for v in raised]
    prob_bf = [v.astype(BF) for v in prob]
    weighted = [prob[h] * grad_prob[h] for h in heads]
    gs = [w - p * jnp.sum(w, axis=-1, keepdims=True) for w, p in zip(weighted, prob)]
    for h in heads:
        gs_out[h] = gs[h]
    gs = [v.astype(BF) for v in gs]
    attended = over_heads(prob_bf, by_head(value))
    dv = dot_cols(stack(prob_bf), grads)
    dq = over_heads(gs, by_head(key))
    dk = dot_cols(stack(gs), queries)
    joint = jnp.concatenate(
        [(dq * scaling).astype(BF), dk.astype(BF), dv.astype(BF)], axis=1
    )
    grad_qkv = dot_cols(hidden, joint)
    grad_proj = dot_cols(attended.astype(BF), g)

    def local():
        grad_hidden = dot_rows(joint, wqkv)
        scaled = grad_hidden * gain
        return (
            inv_std
            * (
                scaled
                - jnp.mean(scaled, axis=-1, keepdims=True)
                - normed * jnp.mean(scaled * normed, axis=-1, keepdims=True)
            )
        ).astype(BF)

    return grad_qkv, grad_proj, local


def pack_weights(grad_qkv, grad_proj, flat, out):
    for c in range(4):
        flat[c * 192 : (c + 1) * 192, :] = grad_qkv[:, c * 128 : (c + 1) * 128]
    flat[768:960, :] = jnp.concatenate([grad_qkv[:, 512:576], grad_proj[:, 128:192]], axis=1)
    flat[960:1152, :] = grad_proj[:, 0:128]
    for r in range(2 * INSIDE):
        out[r // INSIDE, r % INSIDE] = flat[ROWS * r : ROWS * (r + 1), :].astype(BF)


def finish_weights(rows, wqkv, gain, flat, out_qkv, out_proj, out_gain):
    for r in range(2 * INSIDE):
        flat[ROWS * r : ROWS * (r + 1), :] = rows[r // INSIDE, r % INSIDE].astype(F32)
    for c in range(4):
        out_qkv[:, c * 128 : (c + 1) * 128] = flat[c * 192 : (c + 1) * 192, :]
    last = flat[768:960, :]
    out_qkv[:, 512:576] = last[:, 0:64]
    out_proj[:, 128:192] = last[:, 64:128]
    out_proj[:, 0:128] = flat[960:1152, :]
    products = out_qkv[...] * wqkv[...].astype(F32)
    hi, lo = split(products)
    ones = jnp.ones((8, 576), BF)
    row = (dot_rows(ones, hi) + dot_rows(ones, lo))[0:1]
    out_gain[...] = (row / gain[...].reshape(1, D)).reshape(D)


def finish_fields(quads, grad_out, out):
    for s in range(4):
        rows = slice(0, 3) if s >= 2 else slice(3, 6)
        cols = slice(0, 6) if s % 2 else slice(6, 12)
        out[rows, cols] = (grad_out[rows, cols].astype(F32) + quads[s].astype(F32)).astype(BF)


def finish_table(rows, out):
    for k in range(26):
        width = min(128, 3312 - 128 * k)
        block = rows[k // 2].astype(F32)[8 * (k % 2) : 8 * (k % 2) + 8]
        for h in range(HEADS):
            out[h, :, 128 * k : 128 * k + width] = block[h : h + 1, 0:width]


def exchange(src_of, recv, group, send_sem, recv_sem):
    size, rank, device_of = group
    for k in range(1, size):
        peer = lax.rem(rank + k, size)
        pltpu.make_async_remote_copy(
            src_ref=src_of(peer),
            dst_ref=recv.at[rank],
            send_sem=send_sem,
            recv_sem=recv_sem,
            device_id=device_of(peer),
            device_id_type=MESH,
        ).start()


def wait_bytes(ref, sem):
    pltpu.make_async_copy(ref, ref, sem).wait()


def arrive(copies):
    for copy in copies:
        copy.wait_recv()


def total_of(recv):
    total = recv[0].astype(F32)
    for k in range(1, recv.shape[0]):
        total = total + recv[k].astype(F32)
    return total


def kernel(
    fields, grad_out, ids_hbm, gain_hbm, wqkv_hbm, wproj_hbm, table_hbm,
    gather_hbm, shear_hbm, row_hbm, lon_hbm,
    out_flat, out_quads, out_table,
    ids, gain, wqkv, wproj, table, gather, shear, row_of, lon_of,
    field_in, grad_in, xs, bias, gs, stacked, ms, tflat, quads_out, quads_in,
    flat, w_out, w_in, w_half, w1, w2_out, w2, w3, t_out, t1, t2_out, t2, t3,
    block_sem, across_sem, out_sem, load_sem, own_sem, halo_send, halo_recv, back_send, back_recv,
    pair_send, pair_recv, w1_send, w1_recv, w2_send, w2_recv, w3_send, w3_recv, w4_send, w4_recv,
    t1_send, t1_recv, t2_send, t2_recv, t3_send, t3_recv,
):
    l, a = lax.axis_index("lon"), lax.axis_index("lat")
    part, block = lax.rem(l, FOUR), l // FOUR
    core, side = lax.rem(part, 2), part // 2
    near_l, far_l = lax.rem(l + 63, 64), lax.rem(l + 1, 64)
    near_a, far_a = lax.rem(a + 7, 8), lax.rem(a + 1, 8)

    inside = (INSIDE, a * 2 + side, lambda r: (block * FOUR + lax.rem(r, 2) * 2 + core, r // 2))
    across = (ACROSS, block, lambda r: (r * FOUR + part, a))
    in_four = (FOUR, part, lambda r: (block * FOUR + r, a))
    barrier = pltpu.get_barrier_semaphore()
    near = ((near_l, a), (l, near_a), (near_l, near_a))
    far = ((far_l, a), (l, far_a), (far_l, far_a))
    beside = [(near_l, a), (far_l, a), near[2], far[2]]
    column = [(l, lax.rem(a + k, 8)) for k in range(1, 8)]
    aside = (block * FOUR + lax.rem(part + 2, FOUR), a)
    partner = (l + 1 - 2 * core, a)
    high, low = block // 4, lax.rem(block, 4)
    lows = [((high * 4 + lax.rem(low + k, 4)) * FOUR + part, a) for k in range(1, 4)]
    highs = [((lax.rem(high + k, 4) * 4 + low) * FOUR + part, a) for k in range(1, 4)]
    entry = highs + lows + column + beside + [aside]
    for device in entry:
        pl.semaphore_signal(barrier, inc=1, device_id=device, device_id_type=MESH)
    pl.semaphore_wait(barrier, len(entry))

    for s in range(1, 4):
        rows = slice(0, 3) if s >= 2 else slice(3, 6)
        cols = slice(0, 6) if s % 2 else slice(6, 12)
        for k, (src, dst) in enumerate(((fields, field_in), (grad_out, grad_in))):
            copy = pltpu.make_async_remote_copy(
                src_ref=src.at[rows, cols],
                dst_ref=dst.at[s],
                send_sem=halo_send.at[k],
                recv_sem=halo_recv.at[k],
                device_id=near[s - 1],
                device_id_type=MESH,
            )
            copy.start()

    loads = []
    pairs = (
        (table_hbm, table), (shear_hbm, shear), (ids_hbm, ids), (row_hbm, row_of), (lon_hbm, lon_of),
        (gather_hbm, gather), (gain_hbm, gain), (wqkv_hbm, wqkv), (wproj_hbm, wproj),
    )
    for k, (src, dst) in enumerate(pairs):
        load = pltpu.make_async_copy(src, dst, load_sem.at[k])
        load.start()
        loads.append(load)
    owns = []
    for k, (src, dst) in enumerate(((fields, field_in), (grad_out, grad_in))):
        own = pltpu.make_async_copy(src.at[3:6, 6:12], dst.at[0], own_sem.at[k])
        own.start()
        owns.append(own)
    for device in (aside, partner):
        pl.semaphore_signal(block_sem, inc=1, device_id=device, device_id_type=MESH)
    for device in highs:
        pl.semaphore_signal(across_sem, inc=1, device_id=device, device_id_type=MESH)

    for load in loads:
        load.wait()
    expand_bias(table, shear, xs, bias)
    ids_p, ids_q = window_ids(ids, row_of, lon_of, ms)
    same = ids_p == ids_q
    for h in range(HEADS):
        bias[h] = jnp.where(same, bias[h], -1000000000.0)

    for own in owns:
        own.wait()
    wait_bytes(field_in.at[1:], halo_recv.at[0])
    wait_bytes(grad_in.at[1:], halo_recv.at[1])
    moved = dot(gather[...], field_in[...].reshape(TOK, D)).astype(BF)
    moved_grad = dot(gather[...], grad_in[...].reshape(TOK, D)).astype(BF)
    grad_qkv, grad_proj, local = window_grads(
        moved, moved_grad, gain[...].reshape(1, D), wqkv[...], wproj[...], bias, gs
    )

    pack_weights(grad_qkv, grad_proj, flat, w_out)
    rank = inside[1]
    pl.semaphore_wait(block_sem, 2)
    pl.semaphore_wait(across_sem, 3)
    pair = []
    for k in range(1, 5):
        group = lax.rem(rank // 4 + k, 4)
        four_rows = pl.ds(pl.multiple_of(group * 4, 4), 4)
        copy = pltpu.make_async_remote_copy(
            src_ref=w_out.at[1 - core, four_rows],
            dst_ref=w_in.at[four_rows],
            send_sem=pair_send,
            recv_sem=pair_recv.at[k - 1],
            device_id=partner,
            device_id_type=MESH,
        )
        copy.start()
        pair.append(copy)

    for k in range(1, 5):
        group = lax.rem(rank // 4 + k, 4)
        pair[k - 1].wait_recv()
        for j in range(1, 5):
            slot = group * 4 + lax.rem(rank + j, 4)
            both = (w_out[core, slot].astype(F32) + w_in[slot].astype(F32)).astype(BF)
            if k == 4 and j == 4:
                w1[rank] = both
            else:
                w_half[slot] = both
                pltpu.make_async_remote_copy(
                    src_ref=w_half.at[slot],
                    dst_ref=w1.at[rank],
                    send_sem=w1_send,
                    recv_sem=w1_recv,
                    device_id=inside[2](slot),
                    device_id_type=MESH,
                ).start()

    tflat[...] = jnp.zeros_like(tflat)
    fold_bias(gs, shear, stacked, xs, tflat)
    for r in range(ACROSS):
        if r < 13:
            two = [tflat[:, 256 * r : 256 * r + 128], tflat[:, 256 * r + 128 : 256 * r + 256]]
            t_out[r] = jnp.concatenate(two, axis=0).astype(BF)
        else:
            t_out[r] = jnp.zeros((16, 128), BF)
    exchange(lambda r: t_out.at[r], t1, across, t1_send, t1_recv)
    t1[block] = t_out[block]
    quads = dot_cols(gather[...], local()).astype(BF)
    quads_out[...] = quads.reshape(4, 3, 6, 2, D)
    back = []
    for s in range(1, 4):
        copy = pltpu.make_async_remote_copy(
            src_ref=quads_out.at[s],
            dst_ref=quads_in.at[s],
            send_sem=back_send.at[s],
            recv_sem=back_recv.at[s],
            device_id=far[s - 1],
            device_id_type=MESH,
        )
        copy.start()
        back.append(copy)
    quads_in[0] = quads_out[0]

    wait_bytes(field_in.at[1:], halo_send.at[0])
    wait_bytes(grad_in.at[1:], halo_send.at[1])
    wait_bytes(w_in, pair_send)

    wait_bytes(w1.at[1:], w1_recv)
    mine = total_of(w1).astype(BF)
    w2_out[...] = mine
    w2[block] = mine
    exchange(lambda r: w2_out, w2, across, w2_send, w2_recv)

    wait_bytes(t1.at[1:], t1_recv)
    mine = total_of(t1).astype(BF)
    t2_out[...] = mine
    t2[part] = mine
    exchange(lambda r: t2_out, t2, in_four, t2_send, t2_recv)
    wait_bytes(w1.at[1:], w1_send)
    wait_bytes(t1.at[1:], t1_send)
    arrive(back)
    quads_done = pltpu.make_async_copy(quads_in, out_quads, out_sem.at[1])
    quads_done.start()

    wait_bytes(t2.at[1:], t2_recv)
    t3[block] = total_of(t2).astype(BF)
    exchange(lambda r: t3.at[block], t3, across, t3_send, t3_recv)

    wait_bytes(w2.at[1:], w2_recv)
    w3[core, rank] = total_of(w2).astype(BF)
    exchange(lambda r: w3.at[core, rank], w3.at[core], inside, w3_send, w3_recv.at[rank // 4])
    for copy in back:
        copy.wait_send()
    wait_bytes(w2.at[1:], w2_send)
    wait_bytes(t2.at[1:], t2_send)

    for k in range(1, 5):
        group = lax.rem(rank // 4 + 4 - k, 4)
        wait_bytes(w1.at[0:4] if k < 4 else w1.at[0:3], w3_recv.at[group])
        four_rows = pl.ds(pl.multiple_of(group * 4, 4), 4)
        pltpu.make_async_remote_copy(
            src_ref=w3.at[core, four_rows],
            dst_ref=out_flat.at[core, four_rows],
            send_sem=w4_send,
            recv_sem=w4_recv,
            device_id=partner,
            device_id_type=MESH,
        ).start()
    rows_out = pltpu.make_async_copy(w3.at[core], out_flat.at[core], out_sem.at[2])
    rows_out.start()
    wait_bytes(t3.at[1:], t3_recv)
    table_out = pltpu.make_async_copy(t3, out_table, out_sem.at[0])
    table_out.start()
    wait_bytes(t3.at[1:], t3_send)
    wait_bytes(w1.at[1:], w3_send)
    wait_bytes(w1, w4_recv)
    wait_bytes(w1, w4_send)
    quads_done.wait()
    table_out.wait()
    rows_out.wait()


def finish(rows, quads, trows, grad_out, wqkv, gain, out_f, out_qkv, out_proj, out_gain, out_t, flat):
    finish_weights(rows, wqkv, gain, flat, out_qkv, out_proj, out_gain)
    finish_fields(quads, grad_out, out_f)
    finish_table(trows, out_t)


def body(fields, grad_out, mask_ids, ln_gain, qkv_weight, proj_weight, bias_table):
    consts = [jnp.asarray(v, BF) for v in token_tables()]
    fields = jnp.transpose(fields, (1, 2, 0, 3))
    grad_out = jnp.transpose(grad_out, (1, 2, 0, 3))
    vmem = pl.BlockSpec(memory_space=pltpu.VMEM)
    hbm = pl.BlockSpec(memory_space=pl.ANY)
    dma = pltpu.SemaphoreType.DMA
    scratch = [
        pltpu.VMEM((6, 2, 12), jnp.int32),
        pltpu.VMEM((D,), F32),
        pltpu.VMEM((D, 576), BF),
        pltpu.VMEM((D, D), BF),
        pltpu.VMEM((HEADS, 1, 3312), F32),
        pltpu.VMEM((TOK, TOK), BF),
        pltpu.VMEM((512, 384), BF),
        pltpu.VMEM((TOK, 16), BF),
        pltpu.VMEM((TOK, 128), BF),
        pltpu.VMEM((4, 3, 6, 2, D), BF),
        pltpu.VMEM((4, 3, 6, 2, D), BF),
        pltpu.VMEM((4, 96, 128), F32),
        pltpu.VMEM((HEADS, TOK, TOK), F32),
        pltpu.VMEM((HEADS, TOK, TOK), F32),
        pltpu.VMEM((LON, 72, TOK), F32),
        pltpu.VMEM((16, 128), F32),
        pltpu.VMEM((8, 3328), F32),
        pltpu.VMEM((4, 3, 6, 2, D), BF),
        pltpu.VMEM((4, 3, 6, 2, D), BF),
        pltpu.VMEM((1152, 128), F32),
        pltpu.VMEM((2, INSIDE, ROWS, 128), BF),
        pltpu.VMEM((INSIDE, ROWS, 128), BF),
        pltpu.VMEM((INSIDE, ROWS, 128), BF),
        pltpu.VMEM((INSIDE, ROWS, 128), BF),
        pltpu.VMEM((ROWS, 128), BF),
        pltpu.VMEM((ACROSS, ROWS, 128), BF),
        pltpu.VMEM((2, INSIDE, ROWS, 128), BF),
        pltpu.VMEM((ACROSS, 16, 128), BF),
        pltpu.VMEM((ACROSS, 16, 128), BF),
        pltpu.VMEM((16, 128), BF),
        pltpu.VMEM((FOUR, 16, 128), BF),
        pltpu.VMEM((ACROSS, 16, 128), BF),
        pltpu.SemaphoreType.REGULAR,
        pltpu.SemaphoreType.REGULAR,
        dma((3,)),
        dma((9,)),
        dma((2,)),
        dma((2,)),
        dma((2,)),
        dma((4,)),
        dma((4,)),
        dma,
        dma((4,)),
        *([dma] * 5),
        dma((4,)),
        *([dma] * 8),
    ]
    rows, quads, trows = pl.pallas_call(
        kernel,
        out_shape=(
            jax.ShapeDtypeStruct((2, INSIDE, ROWS, 128), BF),
            jax.ShapeDtypeStruct((4, 3, 6, 2, D), BF),
            jax.ShapeDtypeStruct((ACROSS, 16, 128), BF),
        ),
        in_specs=[hbm] * 11,
        out_specs=(hbm, hbm, hbm),
        scratch_shapes=scratch,
        compiler_params=pltpu.CompilerParams(
            collective_id=0, has_side_effects=True, vmem_limit_bytes=VMEM_LIMIT
        ),
    )(
        fields, grad_out, jnp.transpose(mask_ids, (1, 0, 2)), ln_gain, qkv_weight, proj_weight,
        bias_table.reshape(HEADS, 1, 3312), *consts,
    )
    out_f, out_qkv, out_proj, out_gain, out_t = pl.pallas_call(
        finish,
        out_shape=(
            jax.ShapeDtypeStruct((6, 12, 2, D), BF),
            jax.ShapeDtypeStruct((D, 576), F32),
            jax.ShapeDtypeStruct((D, D), F32),
            jax.ShapeDtypeStruct((D,), F32),
            jax.ShapeDtypeStruct((HEADS, 1, 3312), F32),
        ),
        in_specs=[vmem] * 6,
        out_specs=(vmem,) * 5,
        scratch_shapes=[pltpu.VMEM((1152, 128), F32)],
        compiler_params=pltpu.CompilerParams(vmem_limit_bytes=VMEM_LIMIT),
    )(rows, quads, trows, grad_out, qkv_weight, ln_gain)
    out_f = jnp.transpose(out_f, (2, 0, 1, 3))
    return out_f, out_qkv, out_proj, out_gain, out_t.reshape(1, 1, HEADS, 3312)


def solution(mesh):
    placed = (
        P(None, "lat", "lon", None),
        P(None, "lat", "lon", None),
        P(None, "lat", "lon"),
        P(),
        P(),
        P(),
        P("lat", None, None, None),
    )
    return jax.shard_map(
        body,
        mesh=mesh,
        in_specs=placed,
        out_specs=(P(None, "lat", "lon", None), P(), P(), P(), P("lat", None, None, None)),
        check_vma=False,
    )
```
